512 devices in a mesh: pos: 128 (over y, z, core), mode: 4 (over x).
Axes of the slice: x: 4, y: 4, z: 16, core: 2. Of those that a mesh axis runs over, the one named last changes fastest.
Arguments:
- tiles: float32 [128, 2, 2, 128, 128], P('pos'), may hold values from -5 to 5
- probe: float32 [4, 2, 128, 128], P('mode'), may hold values from -5 to 5
- fresnel_phase: float32 [128, 128], replicated, may hold values from -3.140625 to 3.140625
- offsets: int32 [512, 2], P('pos'), may hold values from 0 to 3968, as said below
- measured: float32 [512, 128, 128], P('pos'), may hold values from 0 to 8
Outputs:
- object_grad: float32 [128, 2, 2, 128, 128], P('pos', None, None, 'mode')
- probe_grad: float32 [4, 2, 128, 128], P('mode')
The draws below stay inside these ranges and needn't reach their ends.
Inputs may be any that keep to these rules, and one draw needn't show every extreme that they name: `offsets`: position q belongs to tile q // 4: its top-left corner lies in that tile, and its whole window lies inside the object.
All inputs are finite; a program needn't handle non-finite values.
Results may differ from the reference program's by a relative error of at most 0.0003.
Values sent between devices are 32-bit elements; how exact they have to be, the bound alone decides.
A program may use at most 64 MiB of HBM per device.

```python
import math
import jax
import jax.numpy as jnp
from jax import lax

PATCH = 128
MODES = 4
SLICES = 2
TILE = 128
TILE_COLS = 4
POS_DEV = 4
TILES = 128
TILE_ROWS = 32
POSITIONS = 512


def draw_offsets(key, part):
    key = jax.random.fold_in(key, 3)
    row_key, col_key = jax.random.split(key)
    order = jnp.arange(POSITIONS)
    owner = order // POS_DEV
    slot = order % POS_DEV
    tile_row = owner // TILE_COLS
    tile_col = owner % TILE_COLS
    row_limit = jnp.where(tile_row == TILE_ROWS - 1, TILE - PATCH + 1, TILE)
    col_limit = jnp.where(tile_col == TILE_COLS - 1, TILE - PATCH + 1, TILE)
    row_draw = jax.random.randint(row_key, (POSITIONS,), 0, row_limit)
    col_draw = jax.random.randint(col_key, (POSITIONS,), 0, col_limit)
    local_row = jnp.where(slot == 0, row_limit - 1, jnp.where(slot == 1, 0, row_draw))
    local_col = jnp.where(slot == 0, col_limit - 1, jnp.where(slot == 1, 0, col_draw))
    rows = tile_row * TILE + local_row
    cols = tile_col * TILE + local_col
    return jnp.stack([rows, cols], axis=1).astype(jnp.int32)


def shard_levels(own_key, shape, pieces, smallest, largest):
    def one(axis_at, parts):
        heights = jax.random.uniform(jax.random.fold_in(jax.random.fold_in(own_key, 6), axis_at), (parts,), jnp.float32, smallest / len(pieces), largest / len(pieces))
        return jnp.repeat(jnp.exp(heights), shape[axis_at] // parts).reshape((-1,) + (1,) * (len(shape) - axis_at - 1))

    gain = one(*pieces[0])
    for cut in pieces[1:]:
        gain = gain * one(*cut)
    return gain


def scatter_about(own_key, dims, spread, bound, cuts=(), kind=jnp.bfloat16):
    drawn = spread * jax.random.normal(own_key, dims, jnp.float32)
    if cuts:
        drawn = drawn * shard_levels(own_key, dims, cuts, -0.22, 0.18)
    return jnp.clip(drawn, -bound, bound).astype(kind)


def setup_inputs(seed: int = 0) -> dict:
    streams_of = jax.random.split(jax.random.key(seed), 6)
    return {
        "tiles": scatter_about(streams_of[0], (TILES, SLICES, 2, TILE, TILE), 0.7, 5.0, ((0, 128),), jnp.float32),
        "probe": scatter_about(streams_of[1], (MODES, 2, PATCH, PATCH), 0.7, 5.0, ((0, 4),), jnp.float32),
        "fresnel_phase": jnp.clip(jax.random.uniform(streams_of[2], (PATCH, PATCH), jnp.float32, -3.140625, 3.140625), -3.140625, 3.140625),
        "offsets": draw_offsets(jax.random.fold_in(streams_of[5], 71), 0),
        "measured": jnp.clip(8.0 * jax.random.uniform(streams_of[4], (POSITIONS, PATCH, PATCH), jnp.float32) ** shard_levels(streams_of[4], (POSITIONS, PATCH, PATCH), ((0, 128),), -0.2, 0.2), 0.0, 8.0),
    }


def tables(size):
    index = jnp.arange(size)
    angle = (index[:, None] * index[None, :] % size).astype(jnp.float32) * (2.0 * math.pi / size)
    factor = 1.0 / math.sqrt(size)
    return (jnp.cos(angle) * factor, jnp.sin(angle) * factor)

def transform(real, imag, cosines, sines, sign):
    highest = lax.Precision.HIGHEST
    signed = sines * sign

    def left_side(table, data):
        return jnp.einsum('jk,...kl->...jl', table, data, precision=highest)

    def right_side(data, table):
        return jnp.einsum('...jk,kl->...jl', data, table, precision=highest)
    first_re = left_side(cosines, real) - left_side(signed, imag)
    first_im = left_side(cosines, imag) + left_side(signed, real)
    out_re = right_side(first_re, cosines) - right_side(first_im, signed)
    out_im = right_side(first_im, cosines) + right_side(first_re, signed)
    return (out_re, out_im)

def complex_mul(a_re, a_im, b_re, b_im):
    return (a_re * b_re - a_im * b_im, a_re * b_im + a_im * b_re)

def conj_mul(a_re, a_im, b_re, b_im):
    return (a_re * b_re + a_im * b_im, a_re * b_im - a_im * b_re)

def reference(tiles, probe, fresnel_phase, offsets, measured):
    cosines, sines = tables(PATCH)
    kernel_re = jnp.cos(fresnel_phase)
    kernel_im = jnp.sin(fresnel_phase)
    image = tiles.reshape(TILE_ROWS, TILE_COLS, SLICES, 2, TILE, TILE).transpose(2, 3, 0, 4, 1, 5)
    image = image.reshape(SLICES, 2, TILE_ROWS * TILE, TILE_COLS * TILE)
    probe_re = probe[:, 0]
    probe_im = probe[:, 1]
    zero = jnp.zeros((), jnp.int32)

    def visit(carry, inputs):
        grad_image, probe_total = carry
        offset, target = inputs
        start = (zero, zero, offset[0].astype(jnp.int32), offset[1].astype(jnp.int32))
        window = lax.dynamic_slice(image, start, (SLICES, 2, PATCH, PATCH))
        front_re, front_im = (window[0, 0], window[0, 1])
        back_re, back_im = (window[1, 0], window[1, 1])
        exit_re, exit_im = complex_mul(probe_re, probe_im, front_re, front_im)
        spec_re, spec_im = transform(exit_re, exit_im, cosines, sines, -1.0)
        spec_re, spec_im = complex_mul(spec_re, spec_im, kernel_re, kernel_im)
        wave_re, wave_im = transform(spec_re, spec_im, cosines, sines, 1.0)
        last_re, last_im = complex_mul(wave_re, wave_im, back_re, back_im)
        far_re, far_im = transform(last_re, last_im, cosines, sines, -1.0)
        intensity = lax.optimization_barrier(jnp.sum(far_re * far_re + far_im * far_im, axis=0))
        resid = intensity - target
        chi_re, chi_im = (resid * far_re, resid * far_im)
        grad_re, grad_im = transform(chi_re, chi_im, cosines, sines, 1.0)
        back_obj_re, back_obj_im = conj_mul(wave_re, wave_im, grad_re, grad_im)
        inner_re, inner_im = conj_mul(back_re, back_im, grad_re, grad_im)
        spec_re, spec_im = transform(inner_re, inner_im, cosines, sines, -1.0)
        spec_re, spec_im = conj_mul(kernel_re, kernel_im, spec_re, spec_im)
        first_re, first_im = transform(spec_re, spec_im, cosines, sines, 1.0)
        front_obj_re, front_obj_im = conj_mul(probe_re, probe_im, first_re, first_im)
        probe_re_term, probe_im_term = conj_mul(front_re, front_im, first_re, first_im)
        terms = jnp.stack([jnp.stack([lax.optimization_barrier(jnp.sum(front_obj_re, axis=0)), lax.optimization_barrier(jnp.sum(front_obj_im, axis=0))]), jnp.stack([lax.optimization_barrier(jnp.sum(back_obj_re, axis=0)), lax.optimization_barrier(jnp.sum(back_obj_im, axis=0))])])
        current = lax.dynamic_slice(grad_image, start, (SLICES, 2, PATCH, PATCH))
        grad_image = lax.dynamic_update_slice(grad_image, current + terms, start)
        probe_total = probe_total + jnp.stack([probe_re_term, probe_im_term], axis=1)
        return ((grad_image, probe_total), None)
    initial = (jnp.zeros(image.shape, jnp.float32), jnp.zeros(probe.shape, jnp.float32))
    (grad_image, probe_total), _ = lax.scan(visit, initial, (offsets, measured))
    object_grad = grad_image.reshape(SLICES, 2, TILE_ROWS, TILE, TILE_COLS, TILE).transpose(2, 4, 0, 1, 3, 5)
    object_grad = object_grad.reshape(TILES, SLICES, 2, TILE, TILE)
    probe_grad = probe_total / math.sqrt(POSITIONS)
    return (object_grad, probe_grad)
```

```python
import math

import jax
import jax.numpy as jnp
import numpy as np
from jax import lax
from jax.experimental import pallas as pl
from jax.experimental.pallas import tpu as pltpu
from jax.sharding import PartitionSpec as P

NX, NY, NZ, NC = 4, 4, 16, 2
NP = NY * NZ * NC
COLS = 4
S = 128
Q = S // NX
F32 = jnp.float32
BF16 = jnp.bfloat16
HALO = (1, COLS, COLS + 1)


def dft_tables():
    k = np.arange(S)
    angle = (np.outer(k, k) % S) * (2.0 * np.pi / S)
    cos, sin = np.cos(angle) / math.sqrt(S), np.sin(angle) / math.sqrt(S)
    fwd = np.block([[cos, -sin], [sin, cos]])
    out = []
    for table in (fwd, fwd.T):
        table = table.astype(np.float32)
        hi = table.astype(BF16)
        lo = (table - hi.astype(np.float32)).astype(BF16)
        out.append(np.stack([hi, lo]))
    return np.stack(out)


def split(x):
    hi = x.astype(BF16)
    return hi, (x - hi.astype(F32)).astype(BF16)


def dot(a, b):
    return jnp.dot(a, b, preferred_element_type=F32)


def mul(a, b):
    return a[0] * b[0] - a[1] * b[1], a[0] * b[1] + a[1] * b[0]


def cmul(a, b):
    return a[0] * b[0] + a[1] * b[1], a[0] * b[1] - a[1] * b[0]


def kernel(
    tiles, probe, phase, offs, measured, tables,
    out_obj, out_probe,
    quarter, rows_sel, win, praw, prb, ph, hc, hs, meas, tab, psi, far, obj, rxo, hsend, hown, hrecv,
    pg, rxc, rxy, zs, rxz, gz, pgall,
    load_sem, halo_s, halo_r, a2a_s, a2a_r, pag_s, pag_r, pfw_s, pfw_r,
    oa_s, oa_r, oh_s, oh_r, c_s, c_r, xy_s, xy_r, z_s, z_r, zg_s, zg_r, f_s, f_r,
):
    p = lax.axis_index("pos")
    m = lax.axis_index("mode")
    c = lax.rem(p, NC)
    z = lax.rem(p // NC, NZ)
    y = p // (NC * NZ)

    def at(yy, zz, cc):
        return (yy * NZ + zz) * NC + cc

    def pos_plus(d):
        return lax.rem(p + (d + NP), NP)

    def mode_plus(d):
        return lax.rem(m + (d + NX), NX)

    def remote(src, dst, ss, rs, pos, mode):
        return pltpu.make_async_remote_copy(
            src_ref=src, dst_ref=dst, send_sem=ss, recv_sem=rs,
            device_id=(pos, mode), device_id_type=pl.DeviceIdType.MESH,
        )

    def band(k):
        return pl.ds(pl.multiple_of(k * Q, Q), Q)

    mine = band(m)
    loads = [
        pltpu.make_async_copy(tiles.at[0, :, :, mine, :], quarter.at[:, 0], load_sem.at[0]),
        pltpu.make_async_copy(probe.at[0], praw.at[m], load_sem.at[1]),
        pltpu.make_async_copy(phase, ph, load_sem.at[2]),
        pltpu.make_async_copy(measured.at[m], meas, load_sem.at[3]),
        pltpu.make_async_copy(tables, tab, load_sem.at[4]),
    ]
    for copy in loads:
        copy.start()

    partners = []
    for d in HALO:
        partners += [(pos_plus(d), m), (pos_plus(-d), m)]
    for dx in range(NX):
        for dy in range(NY):
            if dx or dy:
                partners.append((at(lax.rem(y + dy, NY), z, c), mode_plus(dx)))
    for d in range(1, NZ):
        partners.append((at(y, lax.rem(z + d, NZ), c), m))
    for dy in range(1, NY):
        partners.append((at(lax.rem(y + dy, NY), z, 1 - c), m))
    barrier = pltpu.get_barrier_semaphore()
    for pos, mode in partners:
        pl.semaphore_signal(barrier, inc=1, device_id=(pos, mode), device_id_type=pl.DeviceIdType.MESH)
    pl.semaphore_wait(barrier, len(partners))

    started = []

    def go(copy):
        copy.start()
        started.append(copy)
        return copy

    halo = [[None] * 3 for _ in range(2)]
    for s in range(2):
        for h in (2, 1, 0):
            halo[s][h] = go(remote(
                tiles.at[0, s, :, mine, :], quarter.at[s, h + 1], halo_s.at[s, h], halo_r.at[s, h],
                pos_plus(-HALO[h]), m,
            ))
        if s == 0:
            pag = [
                go(remote(probe.at[0, c], praw.at[m, c], pag_s.at[d - 1], pag_r.at[d - 1], p, mode_plus(d)))
                for d in range(1, NX)
            ]

    base_row = p // COLS * S
    base_col = lax.rem(p, COLS) * S
    iota_r = lax.broadcasted_iota(jnp.int32, (Q, S), 0) + m * Q
    iota_c = lax.broadcasted_iota(jnp.int32, (Q, S), 1)

    def corner(k):
        return offs[k, 0] - base_row, offs[k, 1] - base_col

    row0, col0 = corner(m)
    row_back, col_back = lax.rem(S - row0, S), lax.rem(S - col0, S)

    loads[2].wait()
    hc[...] = jnp.cos(ph[...])
    hs[...] = jnp.sin(ph[...])
    loads[0].wait()

    a2a = [[None] * 3 for _ in range(2)]

    def window_bands(s):
        for h in range(3):
            halo[s][h].wait_recv()
        for k in range(NX):
            r, cc = corner(k)
            for plane in range(2):
                upper = jnp.where(iota_c >= cc, quarter[s, 0, plane], quarter[s, 1, plane])
                lower = jnp.where(iota_c >= cc, quarter[s, 2, plane], quarter[s, 3, plane])
                rows_sel[s, k, plane] = jnp.where(iota_r >= r, upper, lower)
        for d in range(1, NX):
            k = mode_plus(d)
            a2a[s][d - 1] = go(remote(
                rows_sel.at[s, k], win.at[s, :, mine, :], a2a_s.at[s, d - 1], a2a_r.at[s, d - 1], p, k,
            ))
        win[s, :, mine, :] = rows_sel[s, m]

    window_bands(0)

    loads[1].wait()
    pfw = []
    for d in range(1, NX):
        pag[d - 1].wait_recv()
        k = mode_plus(-d)
        pfw.append(go(remote(
            praw.at[k, c], praw.at[k, c], pfw_s.at[d - 1], pfw_r.at[d - 1], at(y, z, 1 - c), m,
        )))
    window_bands(1)
    for copy in pfw:
        copy.wait_recv()
    for k in range(NX):
        for plane in range(2):
            prb[k, plane] = pltpu.roll(pltpu.roll(praw[k, plane], row0, 0), col0, 1)

    loads[3].wait()
    loads[4].wait()

    def transform(a, b, inverse):
        right, left = (1, 0) if inverse else (0, 1)
        x = jnp.concatenate([jnp.concatenate(a, axis=1), jnp.concatenate(b, axis=1)], axis=0)
        hi, lo = split(x)
        w_hi, w_lo = tab[right, 0], tab[right, 1]
        o = dot(hi, w_hi) + (dot(lo, w_hi) + dot(hi, w_lo))
        x = jnp.concatenate(
            [
                jnp.concatenate([o[:S, :S], o[S:, :S]], axis=1),
                jnp.concatenate([o[:S, S:], o[S:, S:]], axis=1),
            ],
            axis=0,
        )
        hi, lo = split(x)
        w_hi, w_lo = tab[left, 0], tab[left, 1]
        o = dot(w_hi, hi) + (dot(w_hi, lo) + dot(w_lo, hi))
        return (o[:S, :S], o[S:, :S]), (o[:S, S:], o[S:, S:])

    def both(ref, k):
        return ref[k, 0], ref[k, 1]

    def put(ref, k, value):
        ref[k, 0] = value[0]
        ref[k, 1] = value[1]

    pairs = ((0, 1), (2, 3))
    for d in range(1, NX):
        a2a[0][d - 1].wait_recv()
    for pair in pairs:
        spec = transform(*[mul(both(prb, k), both(win, 0)) for k in pair], False)
        wave = transform(*[mul(v, (hc[...], hs[...])) for v in spec], True)
        for k, v in zip(pair, wave):
            put(psi, k, v)
    for d in range(1, NX):
        a2a[1][d - 1].wait_recv()
    for pair in pairs:
        wave = transform(*[mul(both(psi, k), both(win, 1)) for k in pair], False)
        for k, v in zip(pair, wave):
            put(far, k, v)
    total = -meas[...]
    for k in range(NX):
        total = total + (far[k, 0] * far[k, 0] + far[k, 1] * far[k, 1])
    meas[...] = total
    for pair in pairs:
        grad = transform(*[(meas[...] * far[k, 0], meas[...] * far[k, 1]) for k in pair], True)
        for k, v in zip(pair, grad):
            put(far, k, v)

    oa = [[None] * 3 for _ in range(2)]

    def send_object(s):
        for d in range(1, NX):
            k = mode_plus(d)
            oa[s][d - 1] = go(remote(
                obj.at[s, :, band(k), :], rxo.at[s, d - 1], oa_s.at[s, d - 1], oa_r.at[s, d - 1], p, k,
            ))

    terms = [cmul(both(psi, k), both(far, k)) for k in range(NX)]
    for plane in range(2):
        obj[1, plane] = (terms[0][plane] + terms[1][plane]) + (terms[2][plane] + terms[3][plane])
    send_object(1)

    cc_copies = [None] * NX
    for index, pair in enumerate(pairs):
        spec = transform(*[cmul(both(win, 1), both(far, k)) for k in pair], False)
        first = transform(*[cmul((hc[...], hs[...]), v) for v in spec], True)
        for k, v in zip(pair, first):
            put(far, k, v)
            back = cmul(both(win, 0), v)
            for plane in range(2):
                pg[k, plane] = pltpu.roll(pltpu.roll(back[plane], row_back, 0), col_back, 1)
            cc_copies[k] = go(remote(
                pg.at[k, 1 - c], rxc.at[k], c_s.at[k], c_r.at[k], at(y, z, 1 - c), m,
            ))
    terms = [cmul(both(prb, k), both(far, k)) for k in range(NX)]
    for plane in range(2):
        obj[0, plane] = (terms[0][plane] + terms[1][plane]) + (terms[2][plane] + terms[3][plane])
    send_object(0)

    guarded = []

    def guarded_go(cond, make):
        @pl.when(cond)
        def _():
            make().start()

        guarded.append((cond, make))

    for k in range(NX):
        cc_copies[k].wait_recv()
        pg[k, c] = pg[k, c] + rxc[k]
        dx = lax.rem(k - m + NX, NX)
        for dy in range(NY):
            yy = lax.rem(y + dy, NY)

            def make(k=k, dx=dx, dy=dy, yy=yy):
                return remote(
                    pg.at[k, c, band(yy), :], rxy.at[dx, dy], xy_s.at[dx, dy], xy_r.at[dx, dy], at(yy, z, c), k,
                )

            if dy:
                go(make())
            else:
                guarded_go(k != m, make)

    oh = [[None] * 3 for _ in range(2)]

    def spread_object(s):
        for d in range(1, NX):
            oa[s][d - 1].wait_recv()
        sums = [[None, None] for _ in range(4)]
        for d in range(NX):
            r, cc = corner(mode_plus(-d))
            low, high = iota_r >= r, iota_c >= cc
            for plane in range(2):
                v = rxo[s, d - 1, plane] if d else obj[s, plane, mine, :]
                zero = jnp.zeros_like(v)
                upper, lower = jnp.where(low, v, zero), jnp.where(low, zero, v)
                parts = (
                    jnp.where(high, upper, zero), jnp.where(high, zero, upper),
                    jnp.where(high, lower, zero), jnp.where(high, zero, lower),
                )
                for i in range(4):
                    old = sums[i][plane]
                    sums[i][plane] = parts[i] if old is None else old + parts[i]
        for plane in range(2):
            hown[s, plane] = sums[0][plane]
            for h in range(3):
                hsend[s, h, plane] = sums[h + 1][plane]
        for h in (2, 1, 0):
            oh[s][h] = go(remote(
                hsend.at[s, h], hrecv.at[s, h], oh_s.at[s, h], oh_r.at[s, h], pos_plus(HALO[h]), m,
            ))

    spread_object(1)
    spread_object(0)

    def wait_recv_xy(dx, dy):
        remote(rxy.at[dx, dy], rxy.at[dx, dy], xy_s.at[dx, dy], xy_r.at[dx, dy], p, m).wait_recv()

    part = pg[m, c, band(y), :]
    for dx in range(NX):
        for dy in range(NY):
            if dx or dy:
                wait_recv_xy(dx, dy)
                part = part + rxy[dx, dy]
    for i in range(4):
        zs[i] = part[8 * i : 8 * i + 8]

    owner = lax.rem(z, 4) == 0
    own = z // 4
    for i in range(4):
        d = lax.rem(4 * i - z + NZ, NZ)

        def make(i=i, d=d):
            return remote(zs.at[i], rxz.at[d], z_s.at[i], z_r.at[d], at(y, 4 * i, c), m)

        guarded_go(z != 4 * i, make)

    def z_gather(d):
        return remote(gz.at[own], gz.at[own], zg_s.at[d], zg_r.at[own], at(y, lax.rem(z + d, NZ), c), m)

    @pl.when(owner)
    def _():
        full = zs[own]
        for d in range(1, NZ):
            remote(rxz.at[d], rxz.at[d], z_s.at[0], z_r.at[d], p, m).wait_recv()
            full = full + rxz[d]
        gz[own] = full * (1.0 / math.sqrt(NX * NP))
        for d in range(1, NZ):
            z_gather(d).start()

    for s in range(2):
        for h in range(3):
            oh[s][h].wait_recv()
        for plane in range(2):
            out_obj[0, s, plane] = (hown[s, plane] + hrecv[s, 0, plane]) + (hrecv[s, 1, plane] + hrecv[s, 2, plane])

    for i in range(4):
        @pl.when(z != 4 * i)
        def _(i=i):
            remote(gz.at[i], gz.at[i], zg_s.at[0], zg_r.at[i], p, m).wait_recv()

    for i in range(4):
        pgall[c, y, i] = gz[i]
    last = []
    for dc in range(NC):
        for dy in range(NY):
            if dc or dy:
                yy = lax.rem(y + dy, NY)
                cc = lax.rem(c + dc, NC)
                last.append(go(remote(
                    gz, pgall.at[c, y], f_s.at[dc, dy], f_r.at[dc, dy], at(yy, z, cc), m,
                )))
    for copy in last:
        copy.wait_recv()
    for plane in range(2):
        for yy in range(NY):
            for i in range(4):
                out_probe[0, plane, yy * Q + 8 * i : yy * Q + 8 * i + 8] = pgall[plane, yy, i]

    for copy in started:
        copy.wait_send()
    for cond, make in guarded:
        @pl.when(cond)
        def _(make=make):
            make().wait_send()

    @pl.when(owner)
    def _():
        for d in range(1, NZ):
            z_gather(d).wait_send()


def body(tables, tiles, probe, phase, offs, measured):
    any_space = pl.BlockSpec(memory_space=pl.ANY)
    vmem = pltpu.VMEM
    dma = pltpu.SemaphoreType.DMA
    return pl.pallas_call(
        kernel,
        out_shape=(
            jax.ShapeDtypeStruct((1, 2, 2, Q, S), F32),
            jax.ShapeDtypeStruct((1, 2, S, S), F32),
        ),
        in_specs=[any_space, any_space, any_space, pl.BlockSpec(memory_space=pltpu.SMEM), any_space, any_space],
        out_specs=(pl.BlockSpec(memory_space=vmem), pl.BlockSpec(memory_space=vmem)),
        scratch_shapes=[
            vmem((2, 4, 2, Q, S), F32),
            vmem((2, NX, 2, Q, S), F32),
            vmem((2, 2, S, S), F32),
            vmem((NX, 2, S, S), F32),
            vmem((NX, 2, S, S), F32),
            vmem((S, S), F32),
            vmem((S, S), F32),
            vmem((S, S), F32),
            vmem((S, S), F32),
            vmem((2, 2, 2 * S, 2 * S), BF16),
            vmem((NX, 2, S, S), F32),
            vmem((NX, 2, S, S), F32),
            vmem((2, 2, S, S), F32),
            vmem((2, 3, 2, Q, S), F32),
            vmem((2, 3, 2, Q, S), F32),
            vmem((2, 2, Q, S), F32),
            vmem((2, 3, 2, Q, S), F32),
            vmem((NX, 2, S, S), F32),
            vmem((NX, S, S), F32),
            vmem((NX, NY, Q, S), F32),
            vmem((4, 8, S), F32),
            vmem((NZ, 8, S), F32),
            vmem((4, 8, S), F32),
            vmem((NC, NY, 4, 8, S), F32),
            dma((5,)),
            dma((2, 3)), dma((2, 3)), dma((2, 3)), dma((2, 3)),
            dma((3,)), dma((3,)), dma((3,)), dma((3,)),
            dma((2, 3)), dma((2, 3)), dma((2, 3)), dma((2, 3)),
            dma((NX,)), dma((NX,)), dma((NX, NY)), dma((NX, NY)),
            dma((4,)), dma((NZ,)), dma((NZ,)), dma((4,)),
            dma((NC, NY)), dma((NC, NY)),
        ],
        compiler_params=pltpu.CompilerParams(
            collective_id=0, has_side_effects=True, vmem_limit_bytes=32 * 1024 * 1024
        ),
    )(tiles, probe, phase, offs, measured, tables)


def solution(mesh):
    tables = dft_tables()

    def run(tiles, probe, phase, offs, measured):
        return jax.shard_map(
            lambda *args: body(jnp.asarray(tables), *args),
            mesh=mesh,
            in_specs=(
                P("pos", None, None, None, None),
                P("mode", None, None, None),
                P(),
                P("pos", None),
                P("pos", None, None),
            ),
            out_specs=(P("pos", None, None, "mode", None), P("mode", None, None, None)),
            check_vma=False,
        )(tiles, probe, phase, offs, measured)

    return run
```

```python
import math

import jax
import jax.numpy as jnp
import numpy as np
from jax import lax
from jax.experimental import pallas as pl
from jax.experimental.pallas import tpu as pltpu
from jax.sharding import PartitionSpec as P

NX, NY, NZ, NC = 4, 4, 16, 2
NP = NY * NZ * NC
COLS = 4
S = 128
Q = S // NX
F32 = jnp.float32
BF16 = jnp.bfloat16
HALO = (1, COLS, COLS + 1)


def dft_tables():
    k = np.arange(S)
    angle = (np.outer(k, k) % S) * (2.0 * np.pi / S)
    cos, sin = np.cos(angle) / math.sqrt(S), np.sin(angle) / math.sqrt(S)
    fwd = np.block([[cos, -sin], [sin, cos]])
    out = []
    for table in (fwd, fwd.T):
        table = table.astype(np.float32)
        hi = table.astype(BF16)
        lo = (table - hi.astype(np.float32)).astype(BF16)
        out.append(np.stack([hi, lo]))
    return np.stack(out)


def split(x):
    hi = x.astype(BF16)
    return hi, (x - hi.astype(F32)).astype(BF16)


def dot(a, b):
    return jnp.dot(a, b, preferred_element_type=F32)


def mul(a, b):
    return a[0] * b[0] - a[1] * b[1], a[0] * b[1] + a[1] * b[0]


def cmul(a, b):
    return a[0] * b[0] + a[1] * b[1], a[0] * b[1] - a[1] * b[0]


def kernel(
    tiles, probe, phase, corners, measured, tables,
    out_obj, out_probe,
    offs, quarter, rows_sel, win, praw, prb, ph, hc, hs, meas, tab, psi, far, obj, rxo, hsend, hown, hrecv,
    pg, rxc, rxy, zs, pgall,
    load_sem, round1, round2, halo_s, halo_r, halo_f, a2a_s, a2a_r, pag_s, pag_r, pfw_s, pfw_r,
    oa_s, oa_r, oh_s, oh_r, c_s, c_r, xy_s, xy_r, z_s, z_r, f_s, f_r,
):
    p = lax.axis_index("pos")
    m = lax.axis_index("mode")
    c = lax.rem(p, NC)
    z = lax.rem(p // NC, NZ)
    y = p // (NC * NZ)

    def at(yy, zz, cc):
        return (yy * NZ + zz) * NC + cc

    def pos_plus(d):
        return lax.rem(p + (d + NP), NP)

    def mode_plus(d):
        return lax.rem(m + (d + NX), NX)

    def remote(src, dst, ss, rs, pos, mode):
        return pltpu.make_async_remote_copy(
            src_ref=src, dst_ref=dst, send_sem=ss, recv_sem=rs,
            device_id=(pos, mode), device_id_type=pl.DeviceIdType.MESH,
        )

    def band(k):
        return pl.ds(pl.multiple_of(k * Q, Q), Q)

    def signal(sem, targets):
        for pos, mode in targets:
            pl.semaphore_signal(sem, inc=1, device_id=(pos, mode), device_id_type=pl.DeviceIdType.MESH)

    def z_plus(d):
        return lax.rem(z + (d + NZ), NZ)

    z_twin = z + 1 - 2 * lax.rem(z, 2)
    x_partners = [(p, mode_plus(d)) for d in range(1, NX)]
    y_partners = [(at(lax.rem(y + d, NY), z, c), m) for d in range(1, NY)]

    near = [(pos_plus(d), m) for d in (5, 4, 1, -1, -4, -5)] + [(at(y, z_plus(d), c), m) for d in (2, -2)]
    near += [(at(y, z_twin, c), m)] + x_partners + y_partners
    barrier = pltpu.get_barrier_semaphore()
    signal(barrier, near)

    mine = band(m)
    loads = [
        pltpu.make_async_copy(tiles.at[0, :, :, mine, :], quarter.at[:, 0], load_sem.at[0]),
        pltpu.make_async_copy(probe.at[0], praw.at[m], load_sem.at[1]),
        pltpu.make_async_copy(phase, ph, load_sem.at[2]),
        pltpu.make_async_copy(measured.at[m], meas, load_sem.at[3]),
        pltpu.make_async_copy(tables, tab, load_sem.at[4]),
        pltpu.make_async_copy(corners, offs, load_sem.at[5]),
    ]
    for copy in loads:
        copy.start()

    pl.semaphore_wait(barrier, len(near))

    started = []

    def go(copy):
        copy.start()
        started.append(copy)
        return copy

    col = lax.rem(p, COLS)
    guarded = []

    def guarded_go(cond, make):
        @pl.when(cond)
        def _():
            make().start()

        guarded.append((cond, make))

    def halo_copy(s, h):
        return remote(
            tiles.at[0, s, :, mine, :], quarter.at[s, h + 1], halo_s.at[s, h], halo_r.at[s, h], pos_plus(-HALO[h]), m
        )

    def halo_forward(s):
        return remote(
            quarter.at[s, 2], quarter.at[s, 3], halo_f.at[s], halo_r.at[s, 2], at(y, z, 1 - c), m
        )

    def halo_send(s):
        guarded_go(col == 2, lambda: halo_copy(s, 2))
        go(halo_copy(s, 1))
        guarded_go(col > 0, lambda: halo_copy(s, 0))

    def halo_wait(s):
        halo_copy(s, 1).wait_recv()
        guarded_go(c == 1, lambda: halo_forward(s))

        @pl.when(col < 3)
        def _():
            halo_copy(s, 0).wait_recv()
            halo_copy(s, 2).wait_recv()

    halo_send(0)
    pag = [
        go(remote(probe.at[0, c], praw.at[m, c], pag_s.at[d - 1], pag_r.at[d - 1], p, mode_plus(d)))
        for d in range(1, NX)
    ]
    halo_send(1)
    signal(round1, x_partners + [(at(y, z, 1 - c), m)] + [(at(y, z_plus(d), c), m) for d in (2, -2)])

    base_row = p // COLS * S
    base_col = col * S
    iota_r = lax.broadcasted_iota(jnp.int32, (Q, S), 0) + m * Q
    iota_c = lax.broadcasted_iota(jnp.int32, (Q, S), 1)

    def corner(k):
        return offs[0, k] - base_row, offs[1, k] - base_col

    loads[5].wait()
    row0, col0 = corner(m)
    row_back, col_back = lax.rem(S - row0, S), lax.rem(S - col0, S)

    loads[2].wait()
    hc[...] = jnp.cos(ph[...])
    hs[...] = jnp.sin(ph[...])
    loads[0].wait()

    a2a = [[None] * 3 for _ in range(2)]

    def window_bands(s):
        halo_wait(s)
        for k in range(NX):
            r, cc = corner(k)
            for plane in range(2):
                upper = jnp.where(iota_c >= cc, quarter[s, 0, plane], quarter[s, 1, plane])
                lower = jnp.where(iota_c >= cc, quarter[s, 2, plane], quarter[s, 3, plane])
                rows_sel[s, k, plane] = jnp.where(iota_r >= r, upper, lower)
        for d in range(1, NX):
            k = mode_plus(d)
            a2a[s][d - 1] = go(remote(
                rows_sel.at[s, k], win.at[s, :, mine, :], a2a_s.at[s, d - 1], a2a_r.at[s, d - 1], p, k,
            ))
        win[s, :, mine, :] = rows_sel[s, m]

    window_bands(0)
    pl.semaphore_wait(round1, 6)
    signal(round2, [(at(y, z_twin, c), m)] + [(at(y, z_plus(d), c), m) for d in (4, -4)])

    loads[1].wait()
    pfw = []
    for d in range(1, NX):
        pag[d - 1].wait_recv()
        k = mode_plus(-d)
        pfw.append(go(remote(
            praw.at[k, c], praw.at[k, c], pfw_s.at[d - 1], pfw_r.at[d - 1], at(y, z, 1 - c), m,
        )))
    window_bands(1)
    for copy in pfw:
        copy.wait_recv()
    for k in range(NX):
        for plane in range(2):
            prb[k, plane] = pltpu.roll(pltpu.roll(praw[k, plane], row0, 0), col0, 1)

    loads[3].wait()
    loads[4].wait()

    def transform(a, b, inverse):
        right, left = (1, 0) if inverse else (0, 1)
        x = jnp.concatenate([jnp.concatenate(a, axis=1), jnp.concatenate(b, axis=1)], axis=0)
        hi, lo = split(x)
        w_hi, w_lo = tab[right, 0], tab[right, 1]
        o = dot(hi, w_hi) + (dot(lo, w_hi) + dot(hi, w_lo))
        x = jnp.concatenate(
            [
                jnp.concatenate([o[:S, :S], o[S:, :S]], axis=1),
                jnp.concatenate([o[:S, S:], o[S:, S:]], axis=1),
            ],
            axis=0,
        )
        hi, lo = split(x)
        w_hi, w_lo = tab[left, 0], tab[left, 1]
        o = dot(w_hi, hi) + (dot(w_hi, lo) + dot(w_lo, hi))
        return (o[:S, :S], o[S:, :S]), (o[:S, S:], o[S:, S:])

    def both(ref, k):
        return ref[k, 0], ref[k, 1]

    def put(ref, k, value):
        ref[k, 0] = value[0]
        ref[k, 1] = value[1]

    pairs = ((0, 1), (2, 3))
    for d in range(1, NX):
        a2a[0][d - 1].wait_recv()
    for pair in pairs:
        spec = transform(*[mul(both(prb, k), both(win, 0)) for k in pair], False)
        wave = transform(*[mul(v, (hc[...], hs[...])) for v in spec], True)
        for k, v in zip(pair, wave):
            put(psi, k, v)
    for d in range(1, NX):
        a2a[1][d - 1].wait_recv()
    for pair in pairs:
        wave = transform(*[mul(both(psi, k), both(win, 1)) for k in pair], False)
        for k, v in zip(pair, wave):
            put(far, k, v)
    total = -meas[...]
    for k in range(NX):
        total = total + (far[k, 0] * far[k, 0] + far[k, 1] * far[k, 1])
    meas[...] = total
    for pair in pairs:
        grad = transform(*[(meas[...] * far[k, 0], meas[...] * far[k, 1]) for k in pair], True)
        for k, v in zip(pair, grad):
            put(far, k, v)

    oa = [[None] * 3 for _ in range(2)]

    def send_object(s):
        for d in range(1, NX):
            k = mode_plus(d)
            oa[s][d - 1] = go(remote(
                obj.at[s, :, band(k), :], rxo.at[s, d - 1], oa_s.at[s, d - 1], oa_r.at[s, d - 1], p, k,
            ))

    terms = [cmul(both(psi, k), both(far, k)) for k in range(NX)]
    for plane in range(2):
        obj[1, plane] = (terms[0][plane] + terms[1][plane]) + (terms[2][plane] + terms[3][plane])
    send_object(1)

    cc_copies = [None] * NX
    half = lax.rem(z, 2)

    def rows16(yy, zz):
        return pl.ds(pl.multiple_of(yy * Q + zz * 16, 16), 16)

    def send_probe(k):
        cc_copies[k].wait_recv()
        pg[k, c] = pg[k, c] + rxc[k]
        dx = lax.rem(k - m + NX, NX)
        for dz in range(2):
            zz = half if dz == 0 else 1 - half
            for dy in range(NY):
                yy = lax.rem(y + dy, NY)

                def make(dz=dz, dy=dy, zz=zz, yy=yy):
                    return remote(
                        pg.at[k, c, rows16(yy, zz), :], rxy.at[dx, dy, dz], xy_s.at[dx, dy, dz], xy_r.at[dx, dy, dz],
                        at(yy, z if dz == 0 else z_twin, c), k,
                    )

                if dy or dz:
                    go(make())
                else:
                    guarded_go(k != m, make)

    for index, pair in enumerate(pairs):
        spec = transform(*[cmul(both(win, 1), both(far, k)) for k in pair], False)
        if index:
            pl.semaphore_wait(round2, 3)
            for k in pairs[0]:
                send_probe(k)
        first = transform(*[cmul((hc[...], hs[...]), v) for v in spec], True)
        for k, v in zip(pair, first):
            put(far, k, v)
            back = cmul(both(win, 0), v)
            for plane in range(2):
                pg[k, plane] = pltpu.roll(pltpu.roll(back[plane], row_back, 0), col_back, 1)
            cc_copies[k] = go(remote(
                pg.at[k, 1 - c], rxc.at[k], c_s.at[k], c_r.at[k], at(y, z, 1 - c), m,
            ))
    terms = [cmul(both(prb, k), both(far, k)) for k in range(NX)]
    for plane in range(2):
        obj[0, plane] = (terms[0][plane] + terms[1][plane]) + (terms[2][plane] + terms[3][plane])
    send_object(0)
    for k in pairs[1]:
        send_probe(k)

    oh = [[None] * 3 for _ in range(2)]

    def spread_object(s):
        for d in range(1, NX):
            oa[s][d - 1].wait_recv()
        sums = [[None, None] for _ in range(4)]
        for d in range(NX):
            r, cc = corner(mode_plus(-d))
            low, high = iota_r >= r, iota_c >= cc
            for plane in range(2):
                v = rxo[s, d - 1, plane] if d else obj[s, plane, mine, :]
                zero = jnp.zeros_like(v)
                upper, lower = jnp.where(low, v, zero), jnp.where(low, zero, v)
                parts = (
                    jnp.where(high, upper, zero), jnp.where(high, zero, upper),
                    jnp.where(high, lower, zero), jnp.where(high, zero, lower),
                )
                for i in range(4):
                    old = sums[i][plane]
                    sums[i][plane] = parts[i] if old is None else old + parts[i]
        for plane in range(2):
            hown[s, plane] = sums[0][plane]
            for h in range(3):
                hsend[s, h, plane] = sums[h + 1][plane]
        for h in (2, 1, 0):
            def make(h=h):
                return remote(
                    hsend.at[s, h], hrecv.at[s, h], oh_s.at[s, h], oh_r.at[s, h], pos_plus(HALO[h]), m,
                )

            oh[s][h] = make()
            if h == 1:
                go(make())
            else:
                guarded_go(col < 3, make)

    spread_object(1)
    spread_object(0)

    part = pg[m, c, rows16(y, half), :]
    for dx in range(NX):
        for dy in range(NY):
            for dz in range(2):
                if dx or dy or dz:
                    slot = rxy.at[dx, dy, dz]
                    remote(slot, slot, xy_s.at[dx, dy, dz], xy_r.at[dx, dy, dz], *x_partners[0]).wait_recv()
                    part = part + rxy[dx, dy, dz]

    place = z // 2
    zs[place] = part
    far_z = []
    for d in range(1, NZ // 2):
        far_z.append(go(remote(
            zs.at[place], zs.at[place], z_s.at[d], z_r.at[d], at(y, z_plus(2 * d), c), m,
        )))
    for copy in far_z:
        copy.wait_recv()
    full = zs[0]
    for i in range(1, NZ // 2):
        full = full + zs[i]
    pgall[c, y, half] = full * (1.0 / math.sqrt(NX * NP))

    last = []
    for dz in range(2):
        for dy in range(NY):
            for dc in range(NC):
                if dc or dy or dz:
                    own = pgall.at[c, y, half]
                    last.append(go(remote(
                        own, own, f_s.at[dc, dy, dz], f_r.at[dc, dy, dz],
                        at(lax.rem(y + dy, NY), z_twin if dz else z, 1 - c if dc else c), m,
                    )))

    @pl.when(col == 0)
    def _():
        for s in range(2):
            for h in (0, 2):
                hrecv[s, h] = jnp.zeros_like(hrecv[s, h])

    @pl.when(col > 0)
    def _():
        for s in range(2):
            for h in (0, 2):
                oh[s][h].wait_recv()

    for s in range(2):
        oh[s][1].wait_recv()
        for plane in range(2):
            out_obj[0, s, plane] = (hown[s, plane] + hrecv[s, 0, plane]) + (hrecv[s, 1, plane] + hrecv[s, 2, plane])

    for copy in last:
        copy.wait_recv()
    for plane in range(2):
        for yy in range(NY):
            for i in range(2):
                out_probe[0, plane, yy * Q + 16 * i : yy * Q + 16 * i + 16] = pgall[plane, yy, i]

    for copy in started:
        copy.wait_send()
    for cond, make in guarded:
        @pl.when(cond)
        def _(make=make):
            make().wait_send()


def body(tables, tiles, probe, phase, offs, measured):
    any_space = pl.BlockSpec(memory_space=pl.ANY)
    vmem = pltpu.VMEM
    dma = pltpu.SemaphoreType.DMA
    return pl.pallas_call(
        kernel,
        out_shape=(
            jax.ShapeDtypeStruct((1, 2, 2, Q, S), F32),
            jax.ShapeDtypeStruct((1, 2, S, S), F32),
        ),
        in_specs=[any_space] * 6,
        out_specs=(pl.BlockSpec(memory_space=vmem), pl.BlockSpec(memory_space=vmem)),
        scratch_shapes=[
            pltpu.SMEM((2, NX), jnp.int32),
            vmem((2, 4, 2, Q, S), F32),
            vmem((2, NX, 2, Q, S), F32),
            vmem((2, 2, S, S), F32),
            vmem((NX, 2, S, S), F32),
            vmem((NX, 2, S, S), F32),
            vmem((S, S), F32),
            vmem((S, S), F32),
            vmem((S, S), F32),
            vmem((S, S), F32),
            vmem((2, 2, 2 * S, 2 * S), BF16),
            vmem((NX, 2, S, S), F32),
            vmem((NX, 2, S, S), F32),
            vmem((2, 2, S, S), F32),
            vmem((2, 3, 2, Q, S), F32),
            vmem((2, 3, 2, Q, S), F32),
            vmem((2, 2, Q, S), F32),
            vmem((2, 3, 2, Q, S), F32),
            vmem((NX, 2, S, S), F32),
            vmem((NX, S, S), F32),
            vmem((NX, NY, 2, 16, S), F32),
            vmem((NZ // 2, 16, S), F32),
            vmem((NC, NY, 2, 16, S), F32),
            dma((6,)), pltpu.SemaphoreType.REGULAR, pltpu.SemaphoreType.REGULAR,
            dma((2, 3)), dma((2, 3)), dma((2,)), dma((2, 3)), dma((2, 3)),
            dma((3,)), dma((3,)), dma((3,)), dma((3,)),
            dma((2, 3)), dma((2, 3)), dma((2, 3)), dma((2, 3)),
            dma((NX,)), dma((NX,)), dma((NX, NY, 2)), dma((NX, NY, 2)),
            dma((NZ // 2,)), dma((NZ // 2,)), dma((NC, NY, 2)), dma((NC, NY, 2)),
        ],
        compiler_params=pltpu.CompilerParams(
            collective_id=0, has_side_effects=True, vmem_limit_bytes=24 * 1024 * 1024
        ),
    )(*[pltpu.with_memory_space_constraint(v, pltpu.HBM) for v in (tiles, probe, phase, offs.T, measured, tables)])


def solution(mesh):
    tables = dft_tables()

    def run(tiles, probe, phase, offs, measured):
        return jax.shard_map(
            lambda *args: body(jnp.asarray(tables), *args),
            mesh=mesh,
            in_specs=(
                P("pos", None, None, None, None),
                P("mode", None, None, None),
                P(),
                P("pos", None),
                P("pos", None, None),
            ),
            out_specs=(P("pos", None, None, "mode", None), P("mode", None, None, None)),
            check_vma=False,
        )(tiles, probe, phase, offs, measured)

    return run
```

```python
import math

import jax
import jax.numpy as jnp
from jax import lax
from jax.experimental import pallas as pl
from jax.experimental.pallas import tpu as pltpu
from jax.sharding import PartitionSpec as P

NX, NY, NZ, NC = 4, 4, 16, 2
NP = NY * NZ * NC
COLS = 4
S = 128
Q = S // NX
F32 = jnp.float32
BF16 = jnp.bfloat16
CUT = 2
HALO = (1, COLS, COLS + 1)


def split(x):
    hi = x.astype(BF16)
    return hi, (x - hi.astype(F32)).astype(BF16)


def dot(a, b):
    return jnp.dot(a, b, preferred_element_type=F32)


def mul(a, b):
    return a[0] * b[0] - a[1] * b[1], a[0] * b[1] + a[1] * b[0]


def cmul(a, b):
    return a[0] * b[0] + a[1] * b[1], a[0] * b[1] - a[1] * b[0]


def kernel(
    tiles, probe, phase, corners, measured,
    out_obj, out_probe,
    offs, quarter, rows_sel, win, praw, prb, ph, hc, hs, meas, tab, psi, far, obj, rxo, hsend, hown, hrecv,
    pg, rxc, rxy, zs, pgall,
    load_sem, round1, round2, halo_s, below_r, side_r, a2a_s, a2a_r, pag_s, pag_r, pfw_s, pfw_r,
    oa_s, oa_r, oh_s, oh_r, c_s, c_r, xy_s, xy_r, z_s, z_r, f_s, f_r,
):
    p = lax.axis_index("pos")
    m = lax.axis_index("mode")
    c = lax.rem(p, NC)
    z = lax.rem(p // NC, NZ)
    y = p // (NC * NZ)

    def at(yy, zz, cc):
        return (yy * NZ + zz) * NC + cc

    def pos_plus(d):
        return lax.rem(p + (d + NP), NP)

    def mode_plus(d):
        return lax.rem(m + (d + NX), NX)

    def remote(src, dst, ss, rs, pos, mode):
        return pltpu.make_async_remote_copy(
            src_ref=src, dst_ref=dst, send_sem=ss, recv_sem=rs,
            device_id=(pos, mode), device_id_type=pl.DeviceIdType.MESH,
        )

    def arrived(ref, sem):
        remote(ref, ref, sem, sem, *x_partners[0]).wait_recv()

    def sent(ref, sem):
        remote(ref, ref, sem, sem, *x_partners[0]).wait_send()

    def band(k):
        return pl.ds(pl.multiple_of(k * Q, Q), Q)

    def signal(sem, targets):
        for pos, mode in targets:
            pl.semaphore_signal(sem, inc=1, device_id=(pos, mode), device_id_type=pl.DeviceIdType.MESH)

    def z_plus(d):
        return lax.rem(z + (d + NZ), NZ)

    z_twin = z + 1 - 2 * lax.rem(z, 2)
    x_partners = [(p, mode_plus(d)) for d in range(1, NX)]
    y_partners = [(at(lax.rem(y + d, NY), z, c), m) for d in range(1, NY)]

    near = [(pos_plus(d), m) for d in (5, 4, 1, -1, -4, -5)] + [(at(y, z_plus(d), c), m) for d in (2, -2)]
    near += [(at(y, z_twin, c), m)] + x_partners + y_partners
    barrier = pltpu.get_barrier_semaphore()
    signal(barrier, near)

    mine = band(m)
    loads = [
        pltpu.make_async_copy(tiles.at[0, :, :, mine, :], quarter.at[:, 0], load_sem.at[0]),
        pltpu.make_async_copy(probe.at[0], praw.at[m], load_sem.at[1]),
        pltpu.make_async_copy(phase, ph, load_sem.at[2]),
        pltpu.make_async_copy(measured.at[m], meas, load_sem.at[3]),
        pltpu.make_async_copy(corners, offs, load_sem.at[4]),
    ]
    for copy in loads:
        copy.start()

    pl.semaphore_wait(barrier, len(near))

    col = lax.rem(p, COLS)

    loads[0].wait()
    loads[1].wait()
    width = 2 // CUT
    pieces = [(s, pl.ds(i * width, width)) for s in range(2) for i in range(CUT)]

    def halo_send(s, planes):
        i = pieces.index((s, planes))
        for h in (2, 1, 0):
            def start(h=h):
                remote(
                    quarter.at[s, 0, planes], quarter.at[s, h + 1, planes], halo_s.at[h],
                    below_r.at[i] if h == 1 else side_r.at[i], pos_plus(-HALO[h]), m,
                ).start()

            if h == 1:
                start()
            else:
                pl.when(col == 2 if h == 2 else col > 0)(start)

    def halo_wait(s, planes):
        i = pieces.index((s, planes))
        arrived(quarter.at[s, 2, planes], below_r.at[i])

        @pl.when(c == 1)
        def _():
            remote(
                quarter.at[s, 2, planes], quarter.at[s, 3, planes], halo_s.at[3], side_r.at[i], at(y, z, 1 - c), m
            ).start()

        @pl.when(col < 3)
        def _():
            arrived(quarter.at[s, 0:2, planes], side_r.at[i])

    for piece in pieces[:CUT]:
        halo_send(*piece)
    for d in (2, 1, 3):
        remote(praw.at[m, c], praw.at[m, c], pag_s, pag_r, p, mode_plus(d)).start()
    for piece in pieces[CUT:]:
        halo_send(*piece)
    signal(round1, x_partners + [(at(y, z, 1 - c), m)] + [(at(y, z_plus(d), c), m) for d in (2, -2)])

    base_row = p // COLS * S
    base_col = col * S
    iota_r = lax.broadcasted_iota(jnp.int32, (Q, S), 0) + m * Q
    iota_c = lax.broadcasted_iota(jnp.int32, (Q, S), 1)

    def corner(k):
        return offs[0, k] - base_row, offs[1, k] - base_col

    loads[4].wait()
    row0, col0 = corner(m)
    row_back, col_back = lax.rem(S - row0, S), lax.rem(S - col0, S)

    index = lax.broadcasted_iota(jnp.int32, (S, S), 0) * lax.broadcasted_iota(jnp.int32, (S, S), 1)
    angle = lax.rem(index, S).astype(F32) * (2.0 * math.pi / S)
    cos_parts, sin_parts = split(jnp.cos(angle) * S**-0.5), split(jnp.sin(angle) * S**-0.5)
    for i in range(2):
        for t in range(2):
            tab[t, i, :S, :S] = cos_parts[i]
            tab[t, i, S:, S:] = cos_parts[i]
            tab[t, i, S * (1 - t) : S * (2 - t), S * t : S * (t + 1)] = sin_parts[i]
            tab[t, i, S * t : S * (t + 1), S * (1 - t) : S * (2 - t)] = -sin_parts[i]
    loads[2].wait()
    hc[...] = jnp.cos(ph[...])
    hs[...] = jnp.sin(ph[...])

    def window_bands(s, planes):
        halo_wait(s, planes)
        for k in range(NX):
            r, cc = corner(k)
            for plane in range(planes.start, planes.start + planes.size):
                upper = jnp.where(iota_c >= cc, quarter[s, 0, plane], quarter[s, 1, plane])
                lower = jnp.where(iota_c >= cc, quarter[s, 2, plane], quarter[s, 3, plane])
                rows_sel[s, k, plane] = jnp.where(iota_r >= r, upper, lower)
        for d in (2, 1, 3):
            k = mode_plus(d)
            remote(rows_sel.at[s, k, planes], win.at[s, planes, mine, :], a2a_s, a2a_r.at[s], p, k).start()
        win[s, planes, mine, :] = rows_sel[s, m, planes]

    def window_wait(s):
        arrived(win.at[s, :, pl.ds(0, S - Q), :], a2a_r.at[s])

    for piece in pieces[:CUT]:
        window_bands(*piece)
    pl.semaphore_wait(round1, 6)
    signal(round2, [(at(y, z_twin, c), m)] + [(at(y, z_plus(d), c), m) for d in (4, -4)])

    arrived(praw.at[0:3, 0], pag_r)
    for d in range(1, NX):
        k = mode_plus(-d)
        remote(praw.at[k, c], praw.at[k, c], pfw_s, pfw_r, at(y, z, 1 - c), m).start()
    for piece in pieces[CUT:]:
        window_bands(*piece)
    arrived(praw.at[0:3, 0], pfw_r)
    order = (2, 1, 3, 0)
    for k in range(NX):
        for plane in range(2):
            prb[k, plane] = pltpu.roll(pltpu.roll(praw[mode_plus(order[k]), plane], row0, 0), col0, 1)

    loads[3].wait()

    def transform(a, b, inverse):
        right, left = (1, 0) if inverse else (0, 1)
        x = jnp.concatenate([jnp.concatenate(a, axis=1), jnp.concatenate(b, axis=1)], axis=0)
        hi, lo = split(x)
        w_hi, w_lo = tab[right, 0], tab[right, 1]
        o = dot(hi, w_hi) + (dot(lo, w_hi) + dot(hi, w_lo))
        x = jnp.concatenate(
            [
                jnp.concatenate([o[:S, :S], o[S:, :S]], axis=1),
                jnp.concatenate([o[:S, S:], o[S:, S:]], axis=1),
            ],
            axis=0,
        )
        hi, lo = split(x)
        w_hi, w_lo = tab[left, 0], tab[left, 1]
        o = dot(w_hi, hi) + (dot(w_hi, lo) + dot(w_lo, hi))
        return (o[:S, :S], o[S:, :S]), (o[:S, S:], o[S:, S:])

    def both(ref, k):
        return ref[k, 0], ref[k, 1]

    def put(ref, k, value):
        ref[k, 0] = value[0]
        ref[k, 1] = value[1]

    pairs = ((0, 1), (2, 3))
    window_wait(0)
    for pair in pairs:
        spec = transform(*[mul(both(prb, k), both(win, 0)) for k in pair], False)
        wave = transform(*[mul(v, (hc[...], hs[...])) for v in spec], True)
        for k, v in zip(pair, wave):
            put(psi, k, v)
    window_wait(1)
    for pair in pairs:
        wave = transform(*[mul(both(psi, k), both(win, 1)) for k in pair], False)
        for k, v in zip(pair, wave):
            put(far, k, v)
    total = -meas[...]
    for k in range(NX):
        total = total + (far[k, 0] * far[k, 0] + far[k, 1] * far[k, 1])
    meas[...] = total
    for pair in pairs:
        grad = transform(*[(meas[...] * far[k, 0], meas[...] * far[k, 1]) for k in pair], True)
        for k, v in zip(pair, grad):
            put(far, k, v)

    def send_object(s):
        for d in (2, 1, 3):
            k = mode_plus(d)
            remote(obj.at[s, :, band(k), :], rxo.at[s, d - 1], oa_s, oa_r.at[s], p, k).start()

    terms = [cmul(both(psi, k), both(far, k)) for k in range(NX)]
    for plane in range(2):
        obj[1, plane] = (terms[0][plane] + terms[1][plane]) + (terms[2][plane] + terms[3][plane])
    send_object(1)

    half = lax.rem(z, 2)

    def rows16(yy, zz):
        return pl.ds(pl.multiple_of(yy * Q + zz * 16, 16), 16)

    def send_probe(index, pair):
        arrived(rxc.at[pair[0] : pair[1] + 1], c_r.at[index])
        for k in pair:
            pg[k, c] = pg[k, c] + rxc[k]
            dx = order[k]
            for dz in range(2):
                zz = half if dz == 0 else 1 - half
                for dy in range(NY):
                    if dx or dy or dz:
                        yy = lax.rem(y + dy, NY)
                        remote(
                            pg.at[k, c, rows16(yy, zz), :], rxy.at[(dx * NY + dy) * 2 + dz], xy_s, xy_r,
                            at(yy, z_twin if dz else z, c), mode_plus(dx),
                        ).start()

    for index, pair in enumerate(pairs):
        spec = transform(*[cmul(both(win, 1), both(far, k)) for k in pair], False)
        if index:
            pl.semaphore_wait(round2, 3)
            send_probe(0, pairs[0])
        first = transform(*[cmul((hc[...], hs[...]), v) for v in spec], True)
        for k, v in zip(pair, first):
            put(far, k, v)
            back = cmul(both(win, 0), v)
            for plane in range(2):
                pg[k, plane] = pltpu.roll(pltpu.roll(back[plane], row_back, 0), col_back, 1)
            remote(pg.at[k, 1 - c], rxc.at[k], c_s, c_r.at[index], at(y, z, 1 - c), m).start()
    terms = [cmul(both(prb, k), both(far, k)) for k in range(NX)]
    for plane in range(2):
        obj[0, plane] = (terms[0][plane] + terms[1][plane]) + (terms[2][plane] + terms[3][plane])
    send_object(0)
    send_probe(1, pairs[1])

    def spread_object(s):
        arrived(rxo.at[s], oa_r.at[s])
        sums = [[None, None] for _ in range(4)]
        for d in range(NX):
            r, cc = corner(mode_plus(-d))
            low, high = iota_r >= r, iota_c >= cc
            for plane in range(2):
                v = rxo[s, d - 1, plane] if d else obj[s, plane, mine, :]
                zero = jnp.zeros_like(v)
                upper, lower = jnp.where(low, v, zero), jnp.where(low, zero, v)
                parts = (
                    jnp.where(high, upper, zero), jnp.where(high, zero, upper),
                    jnp.where(high, lower, zero), jnp.where(high, zero, lower),
                )
                for i in range(4):
                    old = sums[i][plane]
                    sums[i][plane] = parts[i] if old is None else old + parts[i]
        for plane in range(2):
            hown[s, plane] = sums[0][plane]
            for h in range(3):
                hsend[s, h, plane] = sums[h + 1][plane]
        for h in (2, 1, 0):
            def start(h=h):
                remote(
                    hsend.at[s, h], hrecv.at[h, s], oh_s.at[h], oh_r.at[1 if h == 1 else 0], pos_plus(HALO[h]), m
                ).start()

            if h == 1:
                start()
            else:
                pl.when(col < 3)(start)

    spread_object(1)
    spread_object(0)

    part = pg[order.index(0), c, rows16(y, half), :]
    arrived(rxy.at[1:], xy_r)
    for i in range(1, 2 * NX * NY):
        part = part + rxy[i]

    place = z // 2
    zs[place] = part
    for d in (4, 3, 5, 2, 6, 1, 7):
        remote(zs.at[place], zs.at[place], z_s, z_r, at(y, z_plus(2 * d), c), m).start()
    arrived(zs.at[1:], z_r)
    full = zs[0]
    for i in range(1, NZ // 2):
        full = full + zs[i]
    pgall[c, y, half] = full * (1.0 / math.sqrt(NX * NP))

    own = pgall.at[c, y, half]
    for dy in (2, 1, 3, 0):
        for dz in range(2):
            for dc in range(NC):
                if dc or dy or dz:
                    remote(
                        own, own, f_s, f_r,
                        at(lax.rem(y + dy, NY), z_twin if dz else z, 1 - c if dc else c), m,
                    ).start()

    @pl.when(col == 0)
    def _():
        for h in (0, 2):
            hrecv[h] = jnp.zeros_like(hrecv[h])

    @pl.when(col > 0)
    def _():
        arrived(hrecv.at[0:2], oh_r.at[0])

    arrived(hrecv.at[1], oh_r.at[1])
    for s in range(2):
        for plane in range(2):
            out_obj[0, s, plane] = (hown[s, plane] + hrecv[0, s, plane]) + (hrecv[1, s, plane] + hrecv[2, s, plane])

    arrived(rxy.at[0:15], f_r)
    for plane in range(2):
        for yy in range(NY):
            for i in range(2):
                out_probe[0, plane, yy * Q + 16 * i : yy * Q + 16 * i + 16] = pgall[plane, yy, i]

    sent(quarter.at[:, 0], halo_s.at[1])
    pl.when(col > 0)(lambda: sent(quarter.at[:, 0], halo_s.at[0]))
    pl.when(col == 2)(lambda: sent(quarter.at[:, 0], halo_s.at[2]))
    pl.when(c == 1)(lambda: sent(quarter.at[:, 0], halo_s.at[3]))
    sent(praw.at[0:3, 0], pag_s)
    sent(praw.at[0:3, 0], pfw_s)
    sent(rows_sel.at[:, 0:3], a2a_s)
    sent(rxo, oa_s)
    sent(rxc, c_s)
    sent(hown, oh_s.at[1])

    @pl.when(col < 3)
    def _():
        sent(hown, oh_s.at[0])
        sent(hown, oh_s.at[2])

    sent(rxy.at[1:], xy_s)
    sent(zs.at[1:], z_s)
    sent(rxy.at[0:15], f_s)


def body(tiles, probe, phase, offs, measured):
    any_space = pl.BlockSpec(memory_space=pl.ANY)
    vmem = pltpu.VMEM
    dma = pltpu.SemaphoreType.DMA
    return pl.pallas_call(
        kernel,
        out_shape=(
            jax.ShapeDtypeStruct((1, 2, 2, Q, S), F32),
            jax.ShapeDtypeStruct((1, 2, S, S), F32),
        ),
        in_specs=[any_space] * 5,
        out_specs=(pl.BlockSpec(memory_space=vmem), pl.BlockSpec(memory_space=vmem)),
        scratch_shapes=[
            pltpu.SMEM((2, NX), jnp.int32),
            vmem((2, 4, 2, Q, S), F32),
            vmem((2, NX, 2, Q, S), F32),
            vmem((2, 2, S, S), F32),
            vmem((NX, 2, S, S), F32),
            vmem((NX, 2, S, S), F32),
            vmem((S, S), F32),
            vmem((S, S), F32),
            vmem((S, S), F32),
            vmem((S, S), F32),
            vmem((2, 2, 2 * S, 2 * S), BF16),
            vmem((NX, 2, S, S), F32),
            vmem((NX, 2, S, S), F32),
            vmem((2, 2, S, S), F32),
            vmem((2, 3, 2, Q, S), F32),
            vmem((2, 3, 2, Q, S), F32),
            vmem((2, 2, Q, S), F32),
            vmem((3, 2, 2, Q, S), F32),
            vmem((NX, 2, S, S), F32),
            vmem((NX, S, S), F32),
            vmem((2 * NX * NY, 16, S), F32),
            vmem((NZ // 2, 16, S), F32),
            vmem((NC, NY, 2, 16, S), F32),
            dma((5,)), pltpu.SemaphoreType.REGULAR, pltpu.SemaphoreType.REGULAR,
            dma((4,)), dma((2 * CUT,)), dma((2 * CUT,)), dma, dma((2,)), dma, dma, dma, dma,
            dma, dma((2,)), dma((3,)), dma((2,)), dma, dma((2,)),
            dma, dma, dma, dma, dma, dma,
        ],
        compiler_params=pltpu.CompilerParams(
            collective_id=0, has_side_effects=True, vmem_limit_bytes=24 * 1024 * 1024
        ),
    )(*[pltpu.with_memory_space_constraint(v, pltpu.HBM) for v in (tiles, probe, phase, offs.T, measured)])


def solution(mesh):
    def run(tiles, probe, phase, offs, measured):
        return jax.shard_map(
            body,
            mesh=mesh,
            in_specs=(
                P("pos", None, None, None, None),
                P("mode", None, None, None),
                P(),
                P("pos", None),
                P("pos", None, None),
            ),
            out_specs=(P("pos", None, None, "mode", None), P("mode", None, None, None)),
            check_vma=False,
        )(tiles, probe, phase, offs, measured)

    return run
```

```python
import math

import jax
import jax.numpy as jnp
from jax import lax
from jax.experimental import pallas as pl
from jax.experimental.pallas import tpu as pltpu
from jax.sharding import PartitionSpec as P

NX, NY, NZ, NC = 4, 4, 16, 2
NP = NY * NZ * NC
COLS = 4
S = 128
Q = S // NX
F32 = jnp.float32
BF16 = jnp.bfloat16
CUT = 2
HALO = (1, COLS, COLS + 1)


def split(x):
    hi = x.astype(BF16)
    return hi, (x - hi.astype(F32)).astype(BF16)


def dot(a, b):
    return jnp.dot(a, b, preferred_element_type=F32)


def mul(a, b):
    return a[0] * b[0] - a[1] * b[1], a[0] * b[1] + a[1] * b[0]


def cmul(a, b):
    return a[0] * b[0] + a[1] * b[1], a[0] * b[1] - a[1] * b[0]


def kernel(
    tiles, probe, phase, corners, measured,
    out_obj, out_probe,
    offs, quarter, rows_sel, win, praw, prb, ph, hc, hs, meas, tab, psi, far, obj, rxo, hside, hown, hbelow, hside_in, hbelow_in,
    pg, rxc, rxy, zs, pgall,
    load_sem, round1, round2, halo_s, below_r, side_r, a2a_s, a2a_r, pag_s, pag_r, pfw_s, pfw_r,
    oa_s, oa_r, hs_s, hs_r, hb_s, hb_r, c_s, c_r, xy_s, xy_r, z_s, z_r, f_s, f_r,
):
    p = lax.axis_index("pos")
    m = lax.axis_index("mode")
    c = lax.rem(p, NC)
    z = lax.rem(p // NC, NZ)
    y = p // (NC * NZ)

    def at(yy, zz, cc):
        return (yy * NZ + zz) * NC + cc

    def pos_plus(d):
        return lax.rem(p + (d + NP), NP)

    def mode_plus(d):
        return lax.rem(m + (d + NX), NX)

    def remote(src, dst, ss, rs, pos, mode):
        return pltpu.make_async_remote_copy(
            src_ref=src, dst_ref=dst, send_sem=ss, recv_sem=rs,
            device_id=(pos, mode), device_id_type=pl.DeviceIdType.MESH,
        )

    def arrived(ref, sem):
        remote(ref, ref, sem, sem, *x_partners[0]).wait_recv()

    def sent(ref, sem):
        remote(ref, ref, sem, sem, *x_partners[0]).wait_send()

    def band(k):
        return pl.ds(pl.multiple_of(k * Q, Q), Q)

    def signal(sem, targets):
        for pos, mode in targets:
            pl.semaphore_signal(sem, inc=1, device_id=(pos, mode), device_id_type=pl.DeviceIdType.MESH)

    def z_plus(d):
        return lax.rem(z + (d + NZ), NZ)

    z_twin = z + 1 - 2 * lax.rem(z, 2)
    x_partners = [(p, mode_plus(d)) for d in range(1, NX)]
    y_partners = [(at(lax.rem(y + d, NY), z, c), m) for d in range(1, NY)]

    near = [(pos_plus(d), m) for d in (5, 4, 1, -1, -4, -5)] + [(at(y, z_plus(d), c), m) for d in (2, -2)]
    near += [(at(y, z_twin, c), m)] + x_partners + y_partners
    barrier = pltpu.get_barrier_semaphore()
    signal(barrier, near)

    col = lax.rem(p, COLS)

    @pl.when(col == 0)
    def _():
        hside_in[...] = jnp.zeros_like(hside_in)

    mine = band(m)
    loads = [
        pltpu.make_async_copy(tiles.at[0, :, :, mine, :], quarter.at[:, 0], load_sem.at[0]),
        pltpu.make_async_copy(probe.at[0], praw.at[m], load_sem.at[1]),
        pltpu.make_async_copy(phase, ph, load_sem.at[2]),
        pltpu.make_async_copy(measured.at[m], meas, load_sem.at[3]),
        pltpu.make_async_copy(corners, offs, load_sem.at[4]),
    ]
    for copy in loads:
        copy.start()

    pl.semaphore_wait(barrier, len(near))


    loads[0].wait()
    loads[1].wait()
    width = 2 // CUT
    pieces = [(s, pl.ds(i * width, width)) for s in range(2) for i in range(CUT)]

    def halo_send(s, planes):
        i = pieces.index((s, planes))
        for h in (2, 1, 0):
            def start(h=h):
                remote(
                    quarter.at[s, 0, planes], quarter.at[s, h + 1, planes], halo_s.at[h],
                    below_r.at[i] if h == 1 else side_r.at[i], pos_plus(-HALO[h]), m,
                ).start()

            if h == 1:
                start()
            else:
                pl.when(col == 2 if h == 2 else col > 0)(start)

    def halo_wait(s, planes):
        i = pieces.index((s, planes))
        arrived(quarter.at[s, 2, planes], below_r.at[i])

        @pl.when(c == 1)
        def _():
            remote(
                quarter.at[s, 2, planes], quarter.at[s, 3, planes], halo_s.at[3], side_r.at[i], at(y, z, 1 - c), m
            ).start()

        @pl.when(col < 3)
        def _():
            arrived(quarter.at[s, 0:2, planes], side_r.at[i])

    for piece in pieces[:CUT]:
        halo_send(*piece)
    for d in (2, 1, 3):
        remote(praw.at[m, c], praw.at[m, c], pag_s, pag_r, p, mode_plus(d)).start()
    for piece in pieces[CUT:]:
        halo_send(*piece)
    signal(round1, x_partners + [(at(y, z, 1 - c), m)] + [(at(y, z_plus(d), c), m) for d in (2, -2)])

    base_row = p // COLS * S
    base_col = col * S
    iota_r = lax.broadcasted_iota(jnp.int32, (Q, S), 0) + m * Q
    iota_c = lax.broadcasted_iota(jnp.int32, (Q, S), 1)

    def corner(k):
        return offs[0, k] - base_row, offs[1, k] - base_col

    loads[4].wait()
    row0, col0 = corner(m)
    row_back, col_back = lax.rem(S - row0, S), lax.rem(S - col0, S)

    index = lax.broadcasted_iota(jnp.int32, (S, S), 0) * lax.broadcasted_iota(jnp.int32, (S, S), 1)
    angle = lax.rem(index, S).astype(F32) * (2.0 * math.pi / S)
    cos_parts, sin_parts = split(jnp.cos(angle) * S**-0.5), split(jnp.sin(angle) * S**-0.5)
    for i in range(2):
        for t in range(2):
            tab[t, i, :S, :S] = cos_parts[i]
            tab[t, i, S:, S:] = cos_parts[i]
            tab[t, i, S * (1 - t) : S * (2 - t), S * t : S * (t + 1)] = sin_parts[i]
            tab[t, i, S * t : S * (t + 1), S * (1 - t) : S * (2 - t)] = -sin_parts[i]
    loads[2].wait()
    hc[...] = jnp.cos(ph[...])
    hs[...] = jnp.sin(ph[...])

    def window_bands(s, planes):
        halo_wait(s, planes)
        for k in range(NX):
            r, cc = corner(k)
            for plane in range(planes.start, planes.start + planes.size):
                upper = jnp.where(iota_c >= cc, quarter[s, 0, plane], quarter[s, 1, plane])
                lower = jnp.where(iota_c >= cc, quarter[s, 2, plane], quarter[s, 3, plane])
                rows_sel[s, k, plane] = jnp.where(iota_r >= r, upper, lower)
        for d in (2, 1, 3):
            k = mode_plus(d)
            remote(rows_sel.at[s, k, planes], win.at[s, planes, mine, :], a2a_s, a2a_r.at[s], p, k).start()
        win[s, planes, mine, :] = rows_sel[s, m, planes]

    def window_wait(s):
        arrived(win.at[s, :, pl.ds(0, S - Q), :], a2a_r.at[s])

    for piece in pieces[:CUT]:
        window_bands(*piece)
    pl.semaphore_wait(round1, 6)
    signal(round2, [(at(y, z_twin, c), m)] + [(at(y, z_plus(d), c), m) for d in (4, -4)])

    arrived(praw.at[0:3, 0], pag_r)
    for d in range(1, NX):
        k = mode_plus(-d)
        remote(praw.at[k, c], praw.at[k, c], pfw_s, pfw_r, at(y, z, 1 - c), m).start()
    for piece in pieces[CUT:]:
        window_bands(*piece)
    arrived(praw.at[0:3, 0], pfw_r)
    order = (2, 1, 3, 0)
    for k in range(NX):
        for plane in range(2):
            prb[k, plane] = pltpu.roll(pltpu.roll(praw[mode_plus(order[k]), plane], row0, 0), col0, 1)

    loads[3].wait()

    def transform(groups, inverse):
        right, left = (1, 0) if inverse else (0, 1)
        parts = []
        for a, b in groups:
            x = jnp.concatenate([jnp.concatenate(a, axis=1), jnp.concatenate(b, axis=1)], axis=0)
            parts.append(split(x))
        outs = [dot(hi, tab[right, 0]) + (dot(lo, tab[right, 0]) + dot(hi, tab[right, 1])) for hi, lo in parts]
        parts = []
        for o in outs:
            x = jnp.concatenate(
                [
                    jnp.concatenate([o[:S, :S], o[S:, :S]], axis=1),
                    jnp.concatenate([o[:S, S:], o[S:, S:]], axis=1),
                ],
                axis=0,
            )
            parts.append(split(x))
        outs = [dot(tab[left, 0], hi) + (dot(tab[left, 0], lo) + dot(tab[left, 1], hi)) for hi, lo in parts]
        return [((o[:S, :S], o[S:, :S]), (o[:S, S:], o[S:, S:])) for o in outs]

    def both(ref, k):
        return ref[k, 0], ref[k, 1]

    def put(ref, k, value):
        ref[k, 0] = value[0]
        ref[k, 1] = value[1]

    pairs = ((0, 1), (2, 3))
    window_wait(0)
    specs = transform([[mul(both(prb, k), both(win, 0)) for k in pair] for pair in pairs], False)
    waves = transform([[mul(v, (hc[...], hs[...])) for v in spec] for spec in specs], True)
    for pair, wave in zip(pairs, waves):
        for k, v in zip(pair, wave):
            put(psi, k, v)
    window_wait(1)
    waves = transform([[mul(both(psi, k), both(win, 1)) for k in pair] for pair in pairs], False)
    for pair, wave in zip(pairs, waves):
        for k, v in zip(pair, wave):
            put(far, k, v)
    total = -meas[...]
    for k in range(NX):
        total = total + (far[k, 0] * far[k, 0] + far[k, 1] * far[k, 1])
    meas[...] = total
    grads = transform([[(meas[...] * far[k, 0], meas[...] * far[k, 1]) for k in pair] for pair in pairs], True)
    for pair, grad in zip(pairs, grads):
        for k, v in zip(pair, grad):
            put(far, k, v)

    def send_object(s):
        for d in (2, 1, 3):
            k = mode_plus(d)
            remote(obj.at[s, :, band(k), :], rxo.at[s, d - 1], oa_s, oa_r.at[s], p, k).start()

    terms = [cmul(both(psi, k), both(far, k)) for k in range(NX)]
    for plane in range(2):
        obj[1, plane] = (terms[0][plane] + terms[1][plane]) + (terms[2][plane] + terms[3][plane])
    send_object(1)

    half = lax.rem(z, 2)

    def rows16(yy, zz):
        return pl.ds(pl.multiple_of(yy * Q + zz * 16, 16), 16)

    def send_probe(index, pair):
        arrived(rxc.at[pair[0] : pair[1] + 1], c_r.at[index])
        for k in pair:
            pg[k, c] = pg[k, c] + rxc[k]
            dx = order[k]
            for dz in (1, 0):
                zz = half if dz == 0 else 1 - half
                for dy in (2, 1, 3, 0):
                    if dx or dy or dz:
                        yy = lax.rem(y + dy, NY)
                        remote(
                            pg.at[k, c, rows16(yy, zz), :], rxy.at[(dx * NY + dy) * 2 + dz], xy_s, xy_r,
                            at(yy, z_twin if dz else z, c), mode_plus(dx),
                        ).start()

    specs = transform([[cmul(both(win, 1), both(far, k)) for k in pair] for pair in pairs], False)
    firsts = transform([[cmul((hc[...], hs[...]), v) for v in spec] for spec in specs], True)
    for index, pair in enumerate(pairs):
        first = firsts[index]
        for k, v in zip(pair, first):
            put(far, k, v)
            back = cmul(both(win, 0), v)
            for plane in range(2):
                pg[k, plane] = pltpu.roll(pltpu.roll(back[plane], row_back, 0), col_back, 1)
            remote(pg.at[k, 1 - c], rxc.at[k], c_s, c_r.at[index], at(y, z, 1 - c), m).start()
    pl.semaphore_wait(round2, 3)
    send_probe(0, pairs[0])
    send_probe(1, pairs[1])
    terms = [cmul(both(prb, k), both(far, k)) for k in range(NX)]
    for plane in range(2):
        obj[0, plane] = (terms[0][plane] + terms[1][plane]) + (terms[2][plane] + terms[3][plane])
    send_object(0)

    def spread_object(s):
        arrived(rxo.at[s], oa_r.at[s])
        sums = [[None, None] for _ in range(4)]
        for d in range(NX):
            r, cc = corner(mode_plus(-d))
            low, high = iota_r >= r, iota_c >= cc
            for plane in range(2):
                v = rxo[s, d - 1, plane] if d else obj[s, plane, mine, :]
                zero = jnp.zeros_like(v)
                upper, lower = jnp.where(low, v, zero), jnp.where(low, zero, v)
                parts = (
                    jnp.where(high, upper, zero), jnp.where(high, zero, upper),
                    jnp.where(high, lower, zero), jnp.where(high, zero, lower),
                )
                for i in range(4):
                    old = sums[i][plane]
                    sums[i][plane] = parts[i] if old is None else old + parts[i]
        for plane in range(2):
            hown[s, plane] = sums[0][plane]
            hbelow[s, plane] = sums[2][plane]
            hside[s, 0, plane] = sums[1][plane]
            hside[s, 1, plane] = sums[3][plane]

        @pl.when(col < 3)
        def _():
            remote(hside.at[s], hside_in.at[s], hs_s, hs_r.at[s], pos_plus(1), m).start()

    def send_below(s):
        @pl.when(col > 0)
        def _():
            arrived(hside_in.at[s], hs_r.at[s])

        for plane in range(2):
            hbelow[s, plane] = hbelow[s, plane] + hside_in[s, 1, plane]
        remote(hbelow.at[s], hbelow_in.at[s], hb_s, hb_r, pos_plus(COLS), m).start()

    spread_object(1)

    part = pg[order.index(0), c, rows16(y, half), :]
    arrived(rxy.at[1:], xy_r)
    for i in range(1, 2 * NX * NY):
        part = part + rxy[i]

    place = z // 2
    zs[place] = part
    for d in (4, 3, 5, 2, 6, 1, 7):
        remote(zs.at[place], zs.at[place], z_s, z_r, at(y, z_plus(2 * d), c), m).start()
    send_below(1)
    spread_object(0)
    send_below(0)
    arrived(zs.at[1:], z_r)
    full = zs[0]
    for i in range(1, NZ // 2):
        full = full + zs[i]
    pgall[c, y, half] = full * (1.0 / math.sqrt(NX * NP))

    own = pgall.at[c, y, half]
    for dy in (2, 1, 3, 0):
        for dz in range(2):
            for dc in range(NC):
                if dc or dy or dz:
                    remote(
                        own, own, f_s, f_r,
                        at(lax.rem(y + dy, NY), z_twin if dz else z, 1 - c if dc else c), m,
                    ).start()

    arrived(hbelow_in, hb_r)
    for s in range(2):
        for plane in range(2):
            out_obj[0, s, plane] = hown[s, plane] + hside_in[s, 0, plane] + hbelow_in[s, plane]

    arrived(rxy.at[0:15], f_r)
    for plane in range(2):
        for yy in range(NY):
            for i in range(2):
                out_probe[0, plane, yy * Q + 16 * i : yy * Q + 16 * i + 16] = pgall[plane, yy, i]

    sent(quarter.at[:, 0], halo_s.at[1])
    pl.when(col > 0)(lambda: sent(quarter.at[:, 0], halo_s.at[0]))
    pl.when(col == 2)(lambda: sent(quarter.at[:, 0], halo_s.at[2]))
    pl.when(c == 1)(lambda: sent(quarter.at[:, 0], halo_s.at[3]))
    sent(praw.at[0:3, 0], pag_s)
    sent(praw.at[0:3, 0], pfw_s)
    sent(rows_sel.at[:, 0:3], a2a_s)
    sent(rxo, oa_s)
    sent(rxc, c_s)
    sent(hbelow, hb_s)
    pl.when(col < 3)(lambda: sent(hside, hs_s))
    sent(rxy.at[1:], xy_s)
    sent(zs.at[1:], z_s)
    sent(rxy.at[0:15], f_s)


def body(tiles, probe, phase, offs, measured):
    any_space = pl.BlockSpec(memory_space=pl.ANY)
    vmem = pltpu.VMEM
    dma = pltpu.SemaphoreType.DMA
    return pl.pallas_call(
        kernel,
        out_shape=(
            jax.ShapeDtypeStruct((1, 2, 2, Q, S), F32),
            jax.ShapeDtypeStruct((1, 2, S, S), F32),
        ),
        in_specs=[any_space] * 5,
        out_specs=(pl.BlockSpec(memory_space=vmem), pl.BlockSpec(memory_space=vmem)),
        scratch_shapes=[
            pltpu.SMEM((2, NX), jnp.int32),
            vmem((2, 4, 2, Q, S), F32),
            vmem((2, NX, 2, Q, S), F32),
            vmem((2, 2, S, S), F32),
            vmem((NX, 2, S, S), F32),
            vmem((NX, 2, S, S), F32),
            vmem((S, S), F32),
            vmem((S, S), F32),
            vmem((S, S), F32),
            vmem((S, S), F32),
            vmem((2, 2, 2 * S, 2 * S), BF16),
            vmem((NX, 2, S, S), F32),
            vmem((NX, 2, S, S), F32),
            vmem((2, 2, S, S), F32),
            vmem((2, 3, 2, Q, S), F32),
            vmem((2, 2, 2, Q, S), F32),
            vmem((2, 2, Q, S), F32),
            vmem((2, 2, Q, S), F32),
            vmem((2, 2, 2, Q, S), F32),
            vmem((2, 2, Q, S), F32),
            vmem((NX, 2, S, S), F32),
            vmem((NX, S, S), F32),
            vmem((2 * NX * NY, 16, S), F32),
            vmem((NZ // 2, 16, S), F32),
            vmem((NC, NY, 2, 16, S), F32),
            dma((5,)), pltpu.SemaphoreType.REGULAR, pltpu.SemaphoreType.REGULAR,
            dma((4,)), dma((2 * CUT,)), dma((2 * CUT,)), dma, dma((2,)), dma, dma, dma, dma,
            dma, dma((2,)), dma, dma((2,)), dma, dma, dma, dma((2,)),
            dma, dma, dma, dma, dma, dma,
        ],
        compiler_params=pltpu.CompilerParams(
            collective_id=0, has_side_effects=True, vmem_limit_bytes=24 * 1024 * 1024
        ),
    )(*[pltpu.with_memory_space_constraint(v, pltpu.HBM) for v in (tiles, probe, phase, offs.T, measured)])


def solution(mesh):
    def run(tiles, probe, phase, offs, measured):
        return jax.shard_map(
            body,
            mesh=mesh,
            in_specs=(
                P("pos", None, None, None, None),
                P("mode", None, None, None),
                P(),
                P("pos", None),
                P("pos", None, None),
            ),
            out_specs=(P("pos", None, None, "mode", None), P("mode", None, None, None)),
            check_vma=False,
        )(tiles, probe, phase, offs, measured)

    return run
```

```python
import math

import jax
import jax.numpy as jnp
from jax import lax
from jax.experimental import pallas as pl
from jax.experimental.pallas import tpu as pltpu
from jax.sharding import PartitionSpec as P

NX, NY, NZ, NC = 4, 4, 16, 2
NP = NY * NZ * NC
COLS = 4
S = 128
Q = S // NX
F32 = jnp.float32
BF16 = jnp.bfloat16
CUT = 2
HALO = (1, COLS, COLS + 1)


def split(x):
    hi = x.astype(BF16)
    return hi, (x - hi.astype(F32)).astype(BF16)


def dot(a, b):
    return jnp.dot(a, b, preferred_element_type=F32)


def mul(a, b):
    return a[0] * b[0] - a[1] * b[1], a[0] * b[1] + a[1] * b[0]


def cmul(a, b):
    return a[0] * b[0] + a[1] * b[1], a[0] * b[1] - a[1] * b[0]


def kernel(
    tiles, probe, phase, corners, measured,
    out_obj, out_probe,
    offs, quarter, rows_sel, win, praw, prb, ph, hc, hs, meas, tab, psi, far, obj, rxo, hside, hown, hbelow, hside_in, hbelow_in,
    pg, rxc, rxy, zs, pgall,
    load_sem, round1, round2, halo_s, below_r, side_r, a2a_s, a2a_r, pag_s, pag_r, pfw_s, pfw_r,
    oa_s, oa_r, hs_s, hs_r, hb_s, hb_r, c_s, c_r, xy_s, xy_r, z_s, z_r, f_s, f_r,
):
    p = lax.axis_index("pos")
    m = lax.axis_index("mode")
    c = lax.rem(p, NC)
    z = lax.rem(p // NC, NZ)
    y = p // (NC * NZ)

    def at(yy, zz, cc):
        return (yy * NZ + zz) * NC + cc

    def pos_plus(d):
        return lax.rem(p + (d + NP), NP)

    def mode_plus(d):
        return lax.rem(m + (d + NX), NX)

    def remote(src, dst, ss, rs, pos, mode):
        return pltpu.make_async_remote_copy(
            src_ref=src, dst_ref=dst, send_sem=ss, recv_sem=rs,
            device_id=(pos, mode), device_id_type=pl.DeviceIdType.MESH,
        )

    def arrived(ref, sem):
        remote(ref, ref, sem, sem, *x_partners[0]).wait_recv()

    def sent(ref, sem):
        remote(ref, ref, sem, sem, *x_partners[0]).wait_send()

    def band(k):
        return pl.ds(pl.multiple_of(k * Q, Q), Q)

    def signal(sem, targets):
        for pos, mode in targets:
            pl.semaphore_signal(sem, inc=1, device_id=(pos, mode), device_id_type=pl.DeviceIdType.MESH)

    def z_plus(d):
        return lax.rem(z + (d + NZ), NZ)

    z_twin = z + 1 - 2 * lax.rem(z, 2)
    x_partners = [(p, mode_plus(d)) for d in range(1, NX)]
    y_partners = [(at(lax.rem(y + d, NY), z, c), m) for d in range(1, NY)]

    near = [(pos_plus(d), m) for d in (5, 4, 1, -1, -4, -5)] + [(at(y, z_plus(d), c), m) for d in (2, -2)]
    near += [(at(y, z_twin, c), m)] + x_partners + y_partners
    barrier = pltpu.get_barrier_semaphore()
    signal(barrier, near)

    col = lax.rem(p, COLS)

    @pl.when(col == 0)
    def _():
        hside_in[...] = jnp.zeros_like(hside_in)

    mine = band(m)
    loads = [
        pltpu.make_async_copy(tiles.at[0, :, :, mine, :], quarter.at[:, 0], load_sem.at[0]),
        pltpu.make_async_copy(probe.at[0], praw.at[m], load_sem.at[1]),
        pltpu.make_async_copy(phase, ph, load_sem.at[2]),
        pltpu.make_async_copy(measured.at[m], meas, load_sem.at[3]),
        pltpu.make_async_copy(corners, offs, load_sem.at[4]),
    ]
    for copy in loads:
        copy.start()

    pl.semaphore_wait(barrier, len(near))


    loads[0].wait()
    loads[1].wait()
    width = 2 // CUT
    pieces = [(s, pl.ds(i * width, width)) for s in range(2) for i in range(CUT)]

    def halo_send(s, planes):
        i = pieces.index((s, planes))
        for h in (2, 1, 0):
            def start(h=h):
                remote(
                    quarter.at[s, 0, planes], quarter.at[s, h + 1, planes], halo_s.at[h],
                    below_r.at[i] if h == 1 else side_r.at[i], pos_plus(-HALO[h]), m,
                ).start()

            if h == 1:
                start()
            else:
                pl.when(col == 2 if h == 2 else col > 0)(start)

    def halo_wait(s, planes):
        i = pieces.index((s, planes))
        arrived(quarter.at[s, 2, planes], below_r.at[i])

        @pl.when(c == 1)
        def _():
            remote(
                quarter.at[s, 2, planes], quarter.at[s, 3, planes], halo_s.at[3], side_r.at[i], at(y, z, 1 - c), m
            ).start()

        @pl.when(col < 3)
        def _():
            arrived(quarter.at[s, 0:2, planes], side_r.at[i])

    for piece in pieces[:CUT]:
        halo_send(*piece)
    for d in (2, 1, 3):
        remote(praw.at[m, c], praw.at[m, c], pag_s, pag_r, p, mode_plus(d)).start()
    for piece in pieces[CUT:]:
        halo_send(*piece)
    signal(round1, x_partners + [(at(y, z, 1 - c), m)] + [(at(y, z_plus(d), c), m) for d in (2, -2)])

    base_row = p // COLS * S
    base_col = col * S
    iota_r = lax.broadcasted_iota(jnp.int32, (Q, S), 0) + m * Q
    iota_c = lax.broadcasted_iota(jnp.int32, (Q, S), 1)

    def corner(k):
        return offs[0, k] - base_row, offs[1, k] - base_col

    loads[4].wait()
    row0, col0 = corner(m)
    row_back, col_back = lax.rem(S - row0, S), lax.rem(S - col0, S)

    index = lax.broadcasted_iota(jnp.int32, (S, S), 0) * lax.broadcasted_iota(jnp.int32, (S, S), 1)
    angle = lax.rem(index, S).astype(F32) * (2.0 * math.pi / S)
    cos_parts, sin_parts = split(jnp.cos(angle) * S**-0.5), split(jnp.sin(angle) * S**-0.5)
    for i in range(2):
        for t in range(2):
            tab[t, i, :S, :S] = cos_parts[i]
            tab[t, i, S:, S:] = cos_parts[i]
            tab[t, i, S * (1 - t) : S * (2 - t), S * t : S * (t + 1)] = sin_parts[i]
            tab[t, i, S * t : S * (t + 1), S * (1 - t) : S * (2 - t)] = -sin_parts[i]
    loads[2].wait()
    hc[...] = jnp.cos(ph[...])
    hs[...] = jnp.sin(ph[...])

    def window_bands(s, planes):
        halo_wait(s, planes)
        for k in range(NX):
            r, cc = corner(k)
            for plane in range(planes.start, planes.start + planes.size):
                upper = jnp.where(iota_c >= cc, quarter[s, 0, plane], quarter[s, 1, plane])
                lower = jnp.where(iota_c >= cc, quarter[s, 2, plane], quarter[s, 3, plane])
                rows_sel[s, k, plane] = jnp.where(iota_r >= r, upper, lower)
        for d in (2, 1, 3):
            k = mode_plus(d)
            remote(rows_sel.at[s, k, planes], win.at[s, planes, mine, :], a2a_s, a2a_r.at[s], p, k).start()
        win[s, planes, mine, :] = rows_sel[s, m, planes]

    def window_wait(s):
        arrived(win.at[s, :, pl.ds(0, S - Q), :], a2a_r.at[s])

    for piece in pieces[:CUT]:
        window_bands(*piece)
    pl.semaphore_wait(round1, 6)
    signal(round2, [(at(y, z_twin, c), m)] + [(at(y, z_plus(d), c), m) for d in (4, -4)])

    arrived(praw.at[0:3, 0], pag_r)
    for d in range(1, NX):
        k = mode_plus(-d)
        remote(praw.at[k, c], praw.at[k, c], pfw_s, pfw_r, at(y, z, 1 - c), m).start()
    for piece in pieces[CUT:]:
        window_bands(*piece)
    arrived(praw.at[0:3, 0], pfw_r)
    order = (2, 1, 3, 0)
    for k in range(NX):
        for plane in range(2):
            prb[k, plane] = pltpu.roll(pltpu.roll(praw[mode_plus(order[k]), plane], row0, 0), col0, 1)

    loads[3].wait()

    def transform(groups, inverse):
        right, left = (1, 0) if inverse else (0, 1)

        def first(wave):
            hi, lo = split(jnp.concatenate(wave, axis=1))
            return dot(hi, tab[right, 0]) + (dot(lo, tab[right, 0]) + dot(hi, tab[right, 1]))

        def second(o):
            hi, lo = split(jnp.concatenate(
                [jnp.concatenate([v[:, part * S : (part + 1) * S] for v in o], axis=1) for part in range(2)], axis=0
            ))
            u = []
            for part in range(2):
                rows = slice(part * S, (part + 1) * S)
                u.append(dot(tab[left, 0, rows], hi) + (dot(tab[left, 0, rows], lo) + dot(tab[left, 1, rows], hi)))
            return (u[0][:, :S], u[1][:, :S]), (u[0][:, S:], u[1][:, S:])

        outs = [[first(wave) for wave in group] for group in groups]
        return [second(o) for o in outs]

    def both(ref, k):
        return ref[k, 0], ref[k, 1]

    def put(ref, k, value):
        ref[k, 0] = value[0]
        ref[k, 1] = value[1]

    pairs = ((0, 1), (2, 3))
    window_wait(0)
    specs = transform([[mul(both(prb, k), both(win, 0)) for k in pair] for pair in pairs], False)
    waves = transform([[mul(v, (hc[...], hs[...])) for v in spec] for spec in specs], True)
    for pair, wave in zip(pairs, waves):
        for k, v in zip(pair, wave):
            put(psi, k, v)
    window_wait(1)
    waves = transform([[mul(both(psi, k), both(win, 1)) for k in pair] for pair in pairs], False)
    for pair, wave in zip(pairs, waves):
        for k, v in zip(pair, wave):
            put(far, k, v)
    total = -meas[...]
    for k in range(NX):
        total = total + (far[k, 0] * far[k, 0] + far[k, 1] * far[k, 1])
    meas[...] = total
    grads = transform([[(meas[...] * far[k, 0], meas[...] * far[k, 1]) for k in pair] for pair in pairs], True)
    for pair, grad in zip(pairs, grads):
        for k, v in zip(pair, grad):
            put(far, k, v)

    def send_object(s):
        for d in (2, 1, 3):
            k = mode_plus(d)
            remote(obj.at[s, :, band(k), :], rxo.at[s, d - 1], oa_s, oa_r.at[s], p, k).start()

    terms = [cmul(both(psi, k), both(far, k)) for k in range(NX)]
    for plane in range(2):
        obj[1, plane] = (terms[0][plane] + terms[1][plane]) + (terms[2][plane] + terms[3][plane])
    send_object(1)

    half = lax.rem(z, 2)

    def rows16(yy, zz):
        return pl.ds(pl.multiple_of(yy * Q + zz * 16, 16), 16)

    def send_probe(index, pair):
        arrived(rxc.at[pair[0] : pair[1] + 1], c_r.at[index])
        for k in pair:
            pg[k, c] = pg[k, c] + rxc[k]
            dx = order[k]
            for dz in (1, 0):
                zz = half if dz == 0 else 1 - half
                for dy in (2, 1, 3, 0):
                    if dx or dy or dz:
                        yy = lax.rem(y + dy, NY)
                        remote(
                            pg.at[k, c, rows16(yy, zz), :], rxy.at[(dx * NY + dy) * 2 + dz], xy_s, xy_r,
                            at(yy, z_twin if dz else z, c), mode_plus(dx),
                        ).start()

    specs = transform([[cmul(both(win, 1), both(far, k)) for k in pair] for pair in pairs], False)
    firsts = transform([[cmul((hc[...], hs[...]), v) for v in spec] for spec in specs], True)
    for index, pair in enumerate(pairs):
        first = firsts[index]
        for k, v in zip(pair, first):
            put(far, k, v)
            back = cmul(both(win, 0), v)
            for plane in range(2):
                pg[k, plane] = pltpu.roll(pltpu.roll(back[plane], row_back, 0), col_back, 1)
            remote(pg.at[k, 1 - c], rxc.at[k], c_s, c_r.at[index], at(y, z, 1 - c), m).start()
    pl.semaphore_wait(round2, 3)
    send_probe(0, pairs[0])
    send_probe(1, pairs[1])
    terms = [cmul(both(prb, k), both(far, k)) for k in range(NX)]
    for plane in range(2):
        obj[0, plane] = (terms[0][plane] + terms[1][plane]) + (terms[2][plane] + terms[3][plane])
    send_object(0)

    def spread_object(s):
        arrived(rxo.at[s], oa_r.at[s])
        sums = [[None, None] for _ in range(4)]
        for d in range(NX):
            r, cc = corner(mode_plus(-d))
            low, high = iota_r >= r, iota_c >= cc
            for plane in range(2):
                v = rxo[s, d - 1, plane] if d else obj[s, plane, mine, :]
                zero = jnp.zeros_like(v)
                upper, lower = jnp.where(low, v, zero), jnp.where(low, zero, v)
                parts = (
                    jnp.where(high, upper, zero), jnp.where(high, zero, upper),
                    jnp.where(high, lower, zero), jnp.where(high, zero, lower),
                )
                for i in range(4):
                    old = sums[i][plane]
                    sums[i][plane] = parts[i] if old is None else old + parts[i]
        for plane in range(2):
            hown[s, plane] = sums[0][plane]
            hbelow[s, plane] = sums[2][plane]
            hside[s, 0, plane] = sums[1][plane]
            hside[s, 1, plane] = sums[3][plane]

        @pl.when(col < 3)
        def _():
            remote(hside.at[s], hside_in.at[s], hs_s, hs_r.at[s], pos_plus(1), m).start()

    def send_below(s):
        @pl.when(col > 0)
        def _():
            arrived(hside_in.at[s], hs_r.at[s])

        for plane in range(2):
            hbelow[s, plane] = hbelow[s, plane] + hside_in[s, 1, plane]
        remote(hbelow.at[s], hbelow_in.at[s], hb_s, hb_r, pos_plus(COLS), m).start()

    spread_object(1)

    part = pg[order.index(0), c, rows16(y, half), :]
    arrived(rxy.at[1:], xy_r)
    for i in range(1, 2 * NX * NY):
        part = part + rxy[i]

    place = z // 2
    zs[place] = part
    for d in (4, 3, 5, 2, 6, 1, 7):
        remote(zs.at[place], zs.at[place], z_s, z_r, at(y, z_plus(2 * d), c), m).start()
    send_below(1)
    spread_object(0)
    send_below(0)
    arrived(zs.at[1:], z_r)
    full = zs[0]
    for i in range(1, NZ // 2):
        full = full + zs[i]
    pgall[c, y, half] = full * (1.0 / math.sqrt(NX * NP))

    own = pgall.at[c, y, half]
    for dy in (2, 1, 3, 0):
        for dz in range(2):
            for dc in range(NC):
                if dc or dy or dz:
                    remote(
                        own, own, f_s, f_r,
                        at(lax.rem(y + dy, NY), z_twin if dz else z, 1 - c if dc else c), m,
                    ).start()

    arrived(hbelow_in, hb_r)
    for s in range(2):
        for plane in range(2):
            out_obj[0, s, plane] = hown[s, plane] + hside_in[s, 0, plane] + hbelow_in[s, plane]

    arrived(rxy.at[0:15], f_r)
    for plane in range(2):
        for yy in range(NY):
            for i in range(2):
                out_probe[0, plane, yy * Q + 16 * i : yy * Q + 16 * i + 16] = pgall[plane, yy, i]

    sent(quarter.at[:, 0], halo_s.at[1])
    pl.when(col > 0)(lambda: sent(quarter.at[:, 0], halo_s.at[0]))
    pl.when(col == 2)(lambda: sent(quarter.at[:, 0], halo_s.at[2]))
    pl.when(c == 1)(lambda: sent(quarter.at[:, 0], halo_s.at[3]))
    sent(praw.at[0:3, 0], pag_s)
    sent(praw.at[0:3, 0], pfw_s)
    sent(rows_sel.at[:, 0:3], a2a_s)
    sent(rxo, oa_s)
    sent(rxc, c_s)
    sent(hbelow, hb_s)
    pl.when(col < 3)(lambda: sent(hside, hs_s))
    sent(rxy.at[1:], xy_s)
    sent(zs.at[1:], z_s)
    sent(rxy.at[0:15], f_s)


def body(tiles, probe, phase, offs, measured):
    any_space = pl.BlockSpec(memory_space=pl.ANY)
    vmem = pltpu.VMEM
    dma = pltpu.SemaphoreType.DMA
    return pl.pallas_call(
        kernel,
        out_shape=(
            jax.ShapeDtypeStruct((1, 2, 2, Q, S), F32),
            jax.ShapeDtypeStruct((1, 2, S, S), F32),
        ),
        in_specs=[any_space] * 5,
        out_specs=(pl.BlockSpec(memory_space=vmem), pl.BlockSpec(memory_space=vmem)),
        scratch_shapes=[
            pltpu.SMEM((2, NX), jnp.int32),
            vmem((2, 4, 2, Q, S), F32),
            vmem((2, NX, 2, Q, S), F32),
            vmem((2, 2, S, S), F32),
            vmem((NX, 2, S, S), F32),
            vmem((NX, 2, S, S), F32),
            vmem((S, S), F32),
            vmem((S, S), F32),
            vmem((S, S), F32),
            vmem((S, S), F32),
            vmem((2, 2, 2 * S, 2 * S), BF16),
            vmem((NX, 2, S, S), F32),
            vmem((NX, 2, S, S), F32),
            vmem((2, 2, S, S), F32),
            vmem((2, 3, 2, Q, S), F32),
            vmem((2, 2, 2, Q, S), F32),
            vmem((2, 2, Q, S), F32),
            vmem((2, 2, Q, S), F32),
            vmem((2, 2, 2, Q, S), F32),
            vmem((2, 2, Q, S), F32),
            vmem((NX, 2, S, S), F32),
            vmem((NX, S, S), F32),
            vmem((2 * NX * NY, 16, S), F32),
            vmem((NZ // 2, 16, S), F32),
            vmem((NC, NY, 2, 16, S), F32),
            dma((5,)), pltpu.SemaphoreType.REGULAR, pltpu.SemaphoreType.REGULAR,
            dma((4,)), dma((2 * CUT,)), dma((2 * CUT,)), dma, dma((2,)), dma, dma, dma, dma,
            dma, dma((2,)), dma, dma((2,)), dma, dma, dma, dma((2,)),
            dma, dma, dma, dma, dma, dma,
        ],
        compiler_params=pltpu.CompilerParams(
            collective_id=0, has_side_effects=True, vmem_limit_bytes=24 * 1024 * 1024
        ),
    )(*[pltpu.with_memory_space_constraint(v, pltpu.HBM) for v in (tiles, probe, phase, offs.T, measured)])


def solution(mesh):
    def run(tiles, probe, phase, offs, measured):
        return jax.shard_map(
            body,
            mesh=mesh,
            in_specs=(
                P("pos", None, None, None, None),
                P("mode", None, None, None),
                P(),
                P("pos", None),
                P("pos", None, None),
            ),
            out_specs=(P("pos", None, None, "mode", None), P("mode", None, None, None)),
            check_vma=False,
        )(tiles, probe, phase, offs, measured)

    return run
```

```python
import math

import jax
import jax.numpy as jnp
from jax import lax
from jax.experimental import pallas as pl
from jax.experimental.pallas import tpu as pltpu
from jax.sharding import PartitionSpec as P

NX, NY, NZ, NC = 4, 4, 16, 2
NP = NY * NZ * NC
COLS = 4
S = 128
Q = S // NX
F32 = jnp.float32
BF16 = jnp.bfloat16
CUT = 2
HALO = (1, COLS, COLS + 1)


def split(x):
    hi = x.astype(BF16)
    return hi, (x - hi.astype(F32)).astype(BF16)


def dot(a, b):
    return jnp.dot(a, b, preferred_element_type=F32)


def mul(a, b):
    return a[0] * b[0] - a[1] * b[1], a[0] * b[1] + a[1] * b[0]


def cmul(a, b):
    return a[0] * b[0] + a[1] * b[1], a[0] * b[1] - a[1] * b[0]


def tree_sum(values):
    while len(values) > 1:
        values = [sum(values[i + 1 : i + 2], values[i]) for i in range(0, len(values), 2)]
    return values[0]


def kernel(
    tiles, probe, phase, corners, measured,
    out_obj, out_probe,
    offs, quarter, rows_sel, win, praw, prb, ph, hc, hs, meas, tab, psi, far, obj, rxo, hside, hown, hbelow, hside_in, hbelow_in,
    pg, rxc, rxy, zs, pgall,
    load_sem, round1, round2, halo_s, below_r, side_r, a2a_s, a2a_r, pag_s, pag_r, pfw_s, pfw_r,
    oa_s, oa_r, hs_s, hs_r, hb_s, hb_r, c_s, c_r, xy_s, xy_r, z_s, z_r, f_s, f_r,
):
    p = lax.axis_index("pos")
    m = lax.axis_index("mode")
    c = lax.rem(p, NC)
    z = lax.rem(p // NC, NZ)
    y = p // (NC * NZ)

    def at(yy, zz, cc):
        return (yy * NZ + zz) * NC + cc

    def pos_plus(d):
        return lax.rem(p + (d + NP), NP)

    def mode_plus(d):
        return lax.rem(m + (d + NX), NX)

    def remote(src, dst, ss, rs, pos, mode):
        return pltpu.make_async_remote_copy(
            src_ref=src, dst_ref=dst, send_sem=ss, recv_sem=rs,
            device_id=(pos, mode), device_id_type=pl.DeviceIdType.MESH,
        )

    def arrived(ref, sem):
        remote(ref, ref, sem, sem, *x_partners[0]).wait_recv()

    def sent(ref, sem):
        remote(ref, ref, sem, sem, *x_partners[0]).wait_send()

    def band(k):
        return pl.ds(pl.multiple_of(k * Q, Q), Q)

    def signal(sem, targets):
        for pos, mode in targets:
            pl.semaphore_signal(sem, inc=1, device_id=(pos, mode), device_id_type=pl.DeviceIdType.MESH)

    def z_plus(d):
        return lax.rem(z + (d + NZ), NZ)

    z_twin = z + 1 - 2 * lax.rem(z, 2)
    x_partners = [(p, mode_plus(d)) for d in range(1, NX)]
    y_partners = [(at(lax.rem(y + d, NY), z, c), m) for d in range(1, NY)]

    near = [(pos_plus(d), m) for d in (5, 4, 1, -1, -4, -5)] + [(at(y, z_plus(d), c), m) for d in (2, -2)]
    near += [(at(y, z_twin, c), m)] + x_partners + y_partners
    barrier = pltpu.get_barrier_semaphore()
    signal(barrier, near)

    col = lax.rem(p, COLS)

    @pl.when(col == 0)
    def _():
        hside_in[...] = jnp.zeros_like(hside_in)

    mine = band(m)
    loads = [
        pltpu.make_async_copy(tiles.at[0, :, :, mine, :], quarter.at[:, 0], load_sem.at[0]),
        pltpu.make_async_copy(probe.at[0], praw.at[m], load_sem.at[1]),
        pltpu.make_async_copy(phase, ph, load_sem.at[2]),
        pltpu.make_async_copy(measured.at[m], meas, load_sem.at[3]),
        pltpu.make_async_copy(corners, offs, load_sem.at[4]),
    ]
    for copy in loads:
        copy.start()

    pl.semaphore_wait(barrier, len(near))


    loads[0].wait()
    loads[1].wait()
    width = 2 // CUT
    pieces = [(s, pl.ds(i * width, width)) for s in range(2) for i in range(CUT)]

    def halo_send(s, planes):
        i = pieces.index((s, planes))
        for h in (2, 1, 0):
            def start(h=h):
                remote(
                    quarter.at[s, 0, planes], quarter.at[s, h + 1, planes], halo_s.at[h],
                    below_r.at[i] if h == 1 else side_r.at[i], pos_plus(-HALO[h]), m,
                ).start()

            if h == 1:
                start()
            else:
                pl.when(col == 2 if h == 2 else col > 0)(start)

    def halo_wait(s, planes):
        i = pieces.index((s, planes))
        arrived(quarter.at[s, 2, planes], below_r.at[i])

        @pl.when(c == 1)
        def _():
            remote(
                quarter.at[s, 2, planes], quarter.at[s, 3, planes], halo_s.at[3], side_r.at[i], at(y, z, 1 - c), m
            ).start()

        @pl.when(col < 3)
        def _():
            arrived(quarter.at[s, 0:2, planes], side_r.at[i])

    for piece in pieces[:CUT]:
        halo_send(*piece)
    for d in (2, 1, 3):
        remote(praw.at[m, c], praw.at[m, c], pag_s, pag_r, p, mode_plus(d)).start()
    for piece in pieces[CUT:]:
        halo_send(*piece)
    signal(round1, x_partners + [(at(y, z, 1 - c), m)] + [(at(y, z_plus(d), c), m) for d in (2, -2)])

    base_row = p // COLS * S
    base_col = col * S
    iota_r = lax.broadcasted_iota(jnp.int32, (Q, S), 0) + m * Q
    iota_c = lax.broadcasted_iota(jnp.int32, (Q, S), 1)

    def corner(k):
        return offs[0, k] - base_row, offs[1, k] - base_col

    loads[4].wait()
    row0, col0 = corner(m)
    row_back, col_back = lax.rem(S - row0, S), lax.rem(S - col0, S)

    index = lax.broadcasted_iota(jnp.int32, (S, S), 0) * lax.broadcasted_iota(jnp.int32, (S, S), 1)
    angle = lax.rem(index, S).astype(F32) * (2.0 * math.pi / S)
    cos_parts, sin_parts = split(jnp.cos(angle) * S**-0.5), split(jnp.sin(angle) * S**-0.5)
    for i in range(2):
        for t in range(2):
            tab[t, i, :S, :S] = cos_parts[i]
            tab[t, i, S:, S:] = cos_parts[i]
            tab[t, i, S * (1 - t) : S * (2 - t), S * t : S * (t + 1)] = sin_parts[i]
            tab[t, i, S * t : S * (t + 1), S * (1 - t) : S * (2 - t)] = -sin_parts[i]
    loads[2].wait()
    hc[...] = jnp.cos(ph[...])
    hs[...] = jnp.sin(ph[...])

    def window_bands(s, planes):
        halo_wait(s, planes)
        for k in range(NX):
            r, cc = corner(k)
            for plane in range(planes.start, planes.start + planes.size):
                upper = jnp.where(iota_c >= cc, quarter[s, 0, plane], quarter[s, 1, plane])
                lower = jnp.where(iota_c >= cc, quarter[s, 2, plane], quarter[s, 3, plane])
                rows_sel[s, k, plane] = jnp.where(iota_r >= r, upper, lower)
        for d in (2, 1, 3):
            k = mode_plus(d)
            remote(rows_sel.at[s, k, planes], win.at[s, planes, mine, :], a2a_s, a2a_r.at[s], p, k).start()
        win[s, planes, mine, :] = rows_sel[s, m, planes]

    def window_wait(s):
        arrived(win.at[s, :, pl.ds(0, S - Q), :], a2a_r.at[s])

    for piece in pieces[:CUT]:
        window_bands(*piece)
    pl.semaphore_wait(round1, 6)
    signal(round2, [(at(y, z_twin, c), m)] + [(at(y, z_plus(d), c), m) for d in (4, -4)])

    arrived(praw.at[0:3, 0], pag_r)
    for d in range(1, NX):
        k = mode_plus(-d)
        remote(praw.at[k, c], praw.at[k, c], pfw_s, pfw_r, at(y, z, 1 - c), m).start()
    for piece in pieces[CUT:]:
        window_bands(*piece)
    arrived(praw.at[0:3, 0], pfw_r)
    order = (2, 1, 3, 0)
    for k in range(NX):
        for plane in range(2):
            prb[k, plane] = pltpu.roll(pltpu.roll(praw[mode_plus(order[k]), plane], row0, 0), col0, 1)

    loads[3].wait()

    def transform(groups, inverse):
        right, left = (1, 0) if inverse else (0, 1)

        def first(wave):
            hi, lo = split(jnp.concatenate(wave, axis=1))
            return dot(hi, tab[right, 0]) + (dot(lo, tab[right, 0]) + dot(hi, tab[right, 1]))

        def second(o):
            hi, lo = split(jnp.concatenate(
                [jnp.concatenate([v[:, part * S : (part + 1) * S] for v in o], axis=1) for part in range(2)], axis=0
            ))
            u = []
            for part in range(2):
                rows = slice(part * S, (part + 1) * S)
                u.append(dot(tab[left, 0, rows], hi) + (dot(tab[left, 0, rows], lo) + dot(tab[left, 1, rows], hi)))
            return (u[0][:, :S], u[1][:, :S]), (u[0][:, S:], u[1][:, S:])

        outs = [[first(wave) for wave in group] for group in groups]
        return [second(o) for o in outs]

    def both(ref, k):
        return ref[k, 0], ref[k, 1]

    def put(ref, k, value):
        ref[k, 0] = value[0]
        ref[k, 1] = value[1]

    pairs = ((0, 1), (2, 3))
    window_wait(0)
    specs = transform([[mul(both(prb, k), both(win, 0)) for k in pair] for pair in pairs], False)
    waves = transform([[mul(v, (hc[...], hs[...])) for v in spec] for spec in specs], True)
    for pair, wave in zip(pairs, waves):
        for k, v in zip(pair, wave):
            put(psi, k, v)
    window_wait(1)
    waves = transform([[mul(both(psi, k), both(win, 1)) for k in pair] for pair in pairs], False)
    for pair, wave in zip(pairs, waves):
        for k, v in zip(pair, wave):
            put(far, k, v)
    total = -meas[...]
    for k in range(NX):
        total = total + (far[k, 0] * far[k, 0] + far[k, 1] * far[k, 1])
    meas[...] = total
    grads = transform([[(meas[...] * far[k, 0], meas[...] * far[k, 1]) for k in pair] for pair in pairs], True)
    for pair, grad in zip(pairs, grads):
        for k, v in zip(pair, grad):
            put(far, k, v)

    def send_object(s):
        for d in (2, 1, 3):
            k = mode_plus(d)
            remote(obj.at[s, :, band(k), :], rxo.at[s, d - 1], oa_s, oa_r.at[s], p, k).start()

    terms = [cmul(both(psi, k), both(far, k)) for k in range(NX)]
    for plane in range(2):
        obj[1, plane] = (terms[0][plane] + terms[1][plane]) + (terms[2][plane] + terms[3][plane])
    send_object(1)

    half = lax.rem(z, 2)

    def rows16(yy, zz):
        return pl.ds(pl.multiple_of(yy * Q + zz * 16, 16), 16)

    def send_probe(index, pair):
        arrived(rxc.at[pair[0] : pair[1] + 1], c_r.at[index])
        for k in pair:
            pg[k, c] = pg[k, c] + rxc[k]
            dx = order[k]
            for dz in (1, 0):
                zz = half if dz == 0 else 1 - half
                for dy in (2, 1, 3, 0):
                    if dx or dy or dz:
                        yy = lax.rem(y + dy, NY)
                        remote(
                            pg.at[k, c, rows16(yy, zz), :], rxy.at[(dx * NY + dy) * 2 + dz], xy_s, xy_r,
                            at(yy, z_twin if dz else z, c), mode_plus(dx),
                        ).start()

    specs = transform([[cmul(both(win, 1), both(far, k)) for k in pair] for pair in pairs], False)
    firsts = transform([[cmul((hc[...], hs[...]), v) for v in spec] for spec in specs], True)
    for index, pair in enumerate(pairs):
        first = firsts[index]
        for k, v in zip(pair, first):
            put(far, k, v)
            back = cmul(both(win, 0), v)
            for plane in range(2):
                pg[k, plane] = pltpu.roll(pltpu.roll(back[plane], row_back, 0), col_back, 1)
            remote(pg.at[k, 1 - c], rxc.at[k], c_s, c_r.at[index], at(y, z, 1 - c), m).start()
    pl.semaphore_wait(round2, 3)
    send_probe(0, pairs[0])
    send_probe(1, pairs[1])
    terms = [cmul(both(prb, k), both(far, k)) for k in range(NX)]
    for plane in range(2):
        obj[0, plane] = (terms[0][plane] + terms[1][plane]) + (terms[2][plane] + terms[3][plane])
    send_object(0)

    def spread_object(s):
        arrived(rxo.at[s], oa_r.at[s])
        sums = [[None, None] for _ in range(4)]
        for d in range(NX):
            r, cc = corner(mode_plus(-d))
            low, high = iota_r >= r, iota_c >= cc
            for plane in range(2):
                v = rxo[s, d - 1, plane] if d else obj[s, plane, mine, :]
                zero = jnp.zeros_like(v)
                upper, lower = jnp.where(low, v, zero), jnp.where(low, zero, v)
                parts = (
                    jnp.where(high, upper, zero), jnp.where(high, zero, upper),
                    jnp.where(high, lower, zero), jnp.where(high, zero, lower),
                )
                for i in range(4):
                    old = sums[i][plane]
                    sums[i][plane] = parts[i] if old is None else old + parts[i]
        for plane in range(2):
            hown[s, plane] = sums[0][plane]
            hbelow[s, plane] = sums[2][plane]
            hside[s, 0, plane] = sums[1][plane]
            hside[s, 1, plane] = sums[3][plane]

        @pl.when(col < 3)
        def _():
            remote(hside.at[s], hside_in.at[s], hs_s, hs_r.at[s], pos_plus(1), m).start()

    def send_below(s):
        @pl.when(col > 0)
        def _():
            arrived(hside_in.at[s], hs_r.at[s])

        for plane in range(2):
            hbelow[s, plane] = hbelow[s, plane] + hside_in[s, 1, plane]
        remote(hbelow.at[s], hbelow_in.at[s], hb_s, hb_r, pos_plus(COLS), m).start()

    spread_object(1)

    part = pg[order.index(0), c, rows16(y, half), :]
    arrived(rxy.at[1:], xy_r)
    part = tree_sum([part] + [rxy[i] for i in range(1, 2 * NX * NY)])

    place = z // 2
    zs[place] = part
    for d in (4, 3, 5, 2, 6, 1, 7):
        remote(zs.at[place], zs.at[place], z_s, z_r, at(y, z_plus(2 * d), c), m).start()
    send_below(1)
    spread_object(0)
    send_below(0)
    arrived(zs.at[1:], z_r)
    full = tree_sum([zs[i] for i in range(NZ // 2)])
    pgall[c, y, half] = full * (1.0 / math.sqrt(NX * NP))

    own = pgall.at[c, y, half]
    for dy in (2, 1, 3, 0):
        for dz in range(2):
            for dc in range(NC):
                if dc or dy or dz:
                    remote(
                        own, own, f_s, f_r,
                        at(lax.rem(y + dy, NY), z_twin if dz else z, 1 - c if dc else c), m,
                    ).start()

    arrived(hbelow_in, hb_r)
    for s in range(2):
        for plane in range(2):
            out_obj[0, s, plane] = hown[s, plane] + hside_in[s, 0, plane] + hbelow_in[s, plane]

    arrived(rxy.at[0:15], f_r)
    for plane in range(2):
        for yy in range(NY):
            for i in range(2):
                out_probe[0, plane, yy * Q + 16 * i : yy * Q + 16 * i + 16] = pgall[plane, yy, i]

    sent(quarter.at[:, 0], halo_s.at[1])
    pl.when(col > 0)(lambda: sent(quarter.at[:, 0], halo_s.at[0]))
    pl.when(col == 2)(lambda: sent(quarter.at[:, 0], halo_s.at[2]))
    pl.when(c == 1)(lambda: sent(quarter.at[:, 0], halo_s.at[3]))
    sent(praw.at[0:3, 0], pag_s)
    sent(praw.at[0:3, 0], pfw_s)
    sent(rows_sel.at[:, 0:3], a2a_s)
    sent(rxo, oa_s)
    sent(rxc, c_s)
    sent(hbelow, hb_s)
    pl.when(col < 3)(lambda: sent(hside, hs_s))
    sent(rxy.at[1:], xy_s)
    sent(zs.at[1:], z_s)
    sent(rxy.at[0:15], f_s)


def body(tiles, probe, phase, offs, measured):
    any_space = pl.BlockSpec(memory_space=pl.ANY)
    vmem = pltpu.VMEM
    dma = pltpu.SemaphoreType.DMA
    return pl.pallas_call(
        kernel,
        out_shape=(
            jax.ShapeDtypeStruct((1, 2, 2, Q, S), F32),
            jax.ShapeDtypeStruct((1, 2, S, S), F32),
        ),
        in_specs=[any_space] * 5,
        out_specs=(pl.BlockSpec(memory_space=vmem), pl.BlockSpec(memory_space=vmem)),
        scratch_shapes=[
            pltpu.SMEM((2, NX), jnp.int32),
            vmem((2, 4, 2, Q, S), F32),
            vmem((2, NX, 2, Q, S), F32),
            vmem((2, 2, S, S), F32),
            vmem((NX, 2, S, S), F32),
            vmem((NX, 2, S, S), F32),
            vmem((S, S), F32),
            vmem((S, S), F32),
            vmem((S, S), F32),
            vmem((S, S), F32),
            vmem((2, 2, 2 * S, 2 * S), BF16),
            vmem((NX, 2, S, S), F32),
            vmem((NX, 2, S, S), F32),
            vmem((2, 2, S, S), F32),
            vmem((2, 3, 2, Q, S), F32),
            vmem((2, 2, 2, Q, S), F32),
            vmem((2, 2, Q, S), F32),
            vmem((2, 2, Q, S), F32),
            vmem((2, 2, 2, Q, S), F32),
            vmem((2, 2, Q, S), F32),
            vmem((NX, 2, S, S), F32),
            vmem((NX, S, S), F32),
            vmem((2 * NX * NY, 16, S), F32),
            vmem((NZ // 2, 16, S), F32),
            vmem((NC, NY, 2, 16, S), F32),
            dma((5,)), pltpu.SemaphoreType.REGULAR, pltpu.SemaphoreType.REGULAR,
            dma((4,)), dma((2 * CUT,)), dma((2 * CUT,)), dma, dma((2,)), dma, dma, dma, dma,
            dma, dma((2,)), dma, dma((2,)), dma, dma, dma, dma((2,)),
            dma, dma, dma, dma, dma, dma,
        ],
        compiler_params=pltpu.CompilerParams(
            collective_id=0, has_side_effects=True, vmem_limit_bytes=24 * 1024 * 1024
        ),
    )(*[pltpu.with_memory_space_constraint(v, pltpu.HBM) for v in (tiles, probe, phase, offs.T, measured)])


def solution(mesh):
    def run(tiles, probe, phase, offs, measured):
        return jax.shard_map(
            body,
            mesh=mesh,
            in_specs=(
                P("pos", None, None, None, None),
                P("mode", None, None, None),
                P(),
                P("pos", None),
                P("pos", None, None),
            ),
            out_specs=(P("pos", None, None, "mode", None), P("mode", None, None, None)),
            check_vma=False,
        )(tiles, probe, phase, offs, measured)

    return run
```
